256 devices in a mesh: dp: 64 (over z, x, core), tensor: 4 (over y).
Axes of the slice: x: 4, y: 4, z: 8, core: 2. Of those that a mesh axis runs over, the one named last changes fastest.
Arguments:
- normed_input: bfloat16 [131072, 896], P(('dp', 'tensor')), may hold values from -6 to 6
- grad_query: bfloat16 [131072, 896], P('dp', 'tensor'), may hold values from -6 to 6
- grad_key: bfloat16 [131072, 128], P('dp', 'tensor'), may hold values from -6 to 6
- grad_value: bfloat16 [131072, 128], P('dp', 'tensor'), may hold values from -6 to 6
- context: bfloat16 [131072, 896], P('dp', 'tensor'), may hold values from -6 to 6
- grad_output: bfloat16 [131072, 896], P(('dp', 'tensor')), may hold values from -6 to 6
- w_query: bfloat16 [896, 896], P(None, 'tensor'), may hold values from -0.1875 to 0.1875
- w_key: bfloat16 [896, 128], P(None, 'tensor'), may hold values from -0.1875 to 0.1875
- w_value: bfloat16 [896, 128], P(None, 'tensor'), may hold values from -0.1875 to 0.1875
- w_output: bfloat16 [896, 896], P('tensor'), may hold values from -0.1875 to 0.1875
- error: float32 [57344, 2048], P('dp', 'tensor'), may hold values from -4 to 4
- factor_init: float32 [2048, 32], P('tensor'), may hold values from -1.5 to 3.5
Outputs:
- grad_input: bfloat16 [131072, 896], P(('dp', 'tensor'))
- grad_context: bfloat16 [131072, 896], P('dp', 'tensor')
- new_error: float32 [57344, 2048], P('dp', 'tensor')
- compressed_grad: float32 [896, 2048], P(None, 'tensor')
The draws below stay inside these ranges and needn't reach their ends.
All inputs are finite; a program needn't handle non-finite values.
Results may differ from the reference program's by a relative error of at most 0.00045.
Values may be sent and summed in bfloat16 or wider, within the bound.
A program may use at most 128 MiB of HBM per device.

```python
import jax
import jax.numpy as jnp
from jax import lax

D = 896
KV = 128
RANK = 32
TOK_DEV = 2048
TOKENS = 131072
PACK = 512
ERR_ROWS = 57344
N_DP = 64
N_TENSOR = 4


def draw_factor_init(key, part):
    key = jax.random.fold_in(key, 11)
    total_rows = N_TENSOR * PACK
    noise = 0.5 * jax.random.truncated_normal(key, -3.0, 3.0, (total_rows, RANK), jnp.float32)
    query_cols = D // N_TENSOR
    kv_cols = KV // N_TENSOR
    local_row = jnp.arange(total_rows, dtype=jnp.int32) % PACK
    within = jnp.where(local_row < query_cols, local_row, jnp.where(local_row < query_cols + 2 * kv_cols, local_row - query_cols, local_row - query_cols - 2 * kv_cols))
    marked = within[:, None] % RANK == jnp.arange(RANK, dtype=jnp.int32)[None, :]
    return noise + 2.0 * marked.astype(jnp.float32)


def level_of(rng, dims, pieces, low, largest):
    gain, own = 1.0, jax.random.fold_in(rng, 6)
    for dim, shards_of in pieces:
        heights = jnp.exp(jax.random.uniform(jax.random.fold_in(own, dim), (shards_of,), jnp.float32, low / len(pieces), largest / len(pieces)))
        gain = gain * jnp.repeat(heights, dims[dim] // shards_of).reshape([-1 if axis == dim else 1 for axis in range(len(dims))])
    return gain


def scatter_about(own_key, shape, width, reach, pieces=(), kind=jnp.bfloat16):
    values = width * jax.random.normal(own_key, shape, jnp.float32)
    if pieces:
        values = values * level_of(own_key, shape, pieces, -0.22, 0.18)
    return jnp.clip(values, -reach, reach).astype(kind)


def setup_inputs(seed: int = 0) -> dict:
    key_of = jax.random.split(jax.random.key(seed), 13)
    normed_input = scatter_about(key_of[0], (TOKENS, D), 1.0, 6.0, ((0, 256),))
    grad_query = scatter_about(key_of[1], (TOKENS, D), 1.0, 6.0, ((0, 64), (1, 4)))
    grad_key = scatter_about(key_of[2], (TOKENS, KV), 1.0, 6.0, ((0, 64), (1, 4)))
    grad_value = scatter_about(key_of[3], (TOKENS, KV), 1.0, 6.0, ((0, 64), (1, 4)))
    context = scatter_about(key_of[4], (TOKENS, D), 1.0, 6.0, ((0, 64), (1, 4)))
    grad_output = scatter_about(key_of[5], (TOKENS, D), 1.0, 6.0, ((0, 256),))
    w_query = scatter_about(key_of[6], (D, D), D ** -0.5, 0.1875, ((1, 4),))
    w_key = scatter_about(key_of[7], (D, KV), D ** -0.5, 0.1875, ((1, 4),))
    w_value = scatter_about(key_of[8], (D, KV), D ** -0.5, 0.1875, ((1, 4),))
    w_output = scatter_about(key_of[9], (D, D), D ** -0.5, 0.1875, ((0, 4),))
    error = scatter_about(key_of[10], (ERR_ROWS, N_TENSOR * PACK), 0.5, 4.0, ((0, 64), (1, 4)), jnp.float32)
    factor_init = draw_factor_init(jax.random.fold_in(key_of[12], 71), 0)
    return dict(normed_input=normed_input, grad_query=grad_query, grad_key=grad_key, grad_value=grad_value, context=context, grad_output=grad_output, w_query=w_query, w_key=w_key, w_value=w_value, w_output=w_output, error=error, factor_init=factor_init)


precise = lax.Precision.HIGHEST

def cholesky_basis(left_factor):
    gram_matrix = jnp.einsum('...dr,...ds->...rs', left_factor, left_factor, precision=precise)
    lower_factor = jnp.linalg.cholesky(gram_matrix)
    solved = jax.scipy.linalg.solve_triangular(lower_factor, jnp.swapaxes(left_factor, -1, -2), lower=True)
    return jnp.swapaxes(solved, -1, -2)

def reference(normed_input, grad_query, grad_key, grad_value, context, grad_output, w_query, w_key, w_value, w_output, error, factor_init):
    query_cols = D // N_TENSOR
    kv_cols = KV // N_TENSOR
    grad_scale = float(TOK_DEV) ** (-0.5)
    grad_input = (jnp.dot(grad_query.astype(jnp.float32), w_query.T.astype(jnp.float32), preferred_element_type=jnp.float32) + jnp.dot(grad_key.astype(jnp.float32), w_key.T.astype(jnp.float32), preferred_element_type=jnp.float32) + jnp.dot(grad_value.astype(jnp.float32), w_value.T.astype(jnp.float32), preferred_element_type=jnp.float32)).astype(jnp.bfloat16)
    grad_context = jnp.dot(grad_output.astype(jnp.float32), w_output.T.astype(jnp.float32), preferred_element_type=jnp.float32).astype(jnp.bfloat16)

    def per_replica(replica):
        start_row = (replica * TOK_DEV).astype(jnp.int32)
        inputs_r = lax.dynamic_slice_in_dim(normed_input, start_row, TOK_DEV, 0)
        query_r = lax.dynamic_slice_in_dim(grad_query, start_row, TOK_DEV, 0)
        key_r = lax.dynamic_slice_in_dim(grad_key, start_row, TOK_DEV, 0)
        value_r = lax.dynamic_slice_in_dim(grad_value, start_row, TOK_DEV, 0)
        context_r = lax.dynamic_slice_in_dim(context, start_row, TOK_DEV, 0)
        outgrad_r = lax.dynamic_slice_in_dim(grad_output, start_row, TOK_DEV, 0)
        grad_q = jnp.dot(inputs_r.T.astype(jnp.float32), query_r.astype(jnp.float32), preferred_element_type=jnp.float32)
        grad_k = jnp.dot(inputs_r.T.astype(jnp.float32), key_r.astype(jnp.float32), preferred_element_type=jnp.float32)
        grad_v = jnp.dot(inputs_r.T.astype(jnp.float32), value_r.astype(jnp.float32), preferred_element_type=jnp.float32)
        grad_o = jnp.dot(outgrad_r.T.astype(jnp.float32), context_r.astype(jnp.float32), preferred_element_type=jnp.float32)
        packed = jnp.concatenate((grad_q.reshape(D, N_TENSOR, query_cols), grad_k.reshape(D, N_TENSOR, kv_cols), grad_v.reshape(D, N_TENSOR, kv_cols), grad_o.reshape(D, N_TENSOR, query_cols)), 2)
        error_r = lax.dynamic_slice_in_dim(error, (replica * D).astype(jnp.int32), D, 0)
        return packed * grad_scale + error_r.reshape(D, N_TENSOR, PACK)
    merged = lax.map(per_replica, jnp.arange(N_DP, dtype=jnp.int32))
    factors = factor_init.reshape(N_TENSOR, PACK, RANK)
    edges = ((0, query_cols), (query_cols, query_cols + 2 * kv_cols), (query_cols + 2 * kv_cols, PACK))
    approx_list = []
    compressed_list = []
    for lo_col, hi_col in edges:
        block = merged[..., lo_col:hi_col]
        left_factor = jnp.einsum('ndtc,tcr->tdr', block, factors[:, lo_col:hi_col], precision=precise)
        basis_cols = cholesky_basis(left_factor)
        right_each = jnp.einsum('ndtc,tdr->ntcr', block, basis_cols, precision=precise)
        right_total = jnp.sum(right_each, 0)
        approx_list.append(jnp.einsum('tdr,ntcr->ndtc', basis_cols, right_each, precision=precise))
        compressed_list.append(jnp.einsum('tdr,tcr->dtc', basis_cols, right_total, precision=precise))
    new_error = (merged - jnp.concatenate(approx_list, 3)).reshape(N_DP * D, N_TENSOR * PACK)
    compressed_grad = jnp.concatenate(compressed_list, 2).reshape(D, N_TENSOR * PACK)
    return (grad_input, grad_context, new_error, compressed_grad)
```

```python
import jax
import jax.numpy as jnp
from jax import lax
from jax.experimental import pallas as pl
from jax.experimental.pallas import tpu as pltpu
from jax.sharding import PartitionSpec as P

MESH = pl.DeviceIdType.MESH
F32, BF16 = jnp.float32, jnp.bfloat16
PRECISE = lax.Precision.HIGHEST
NZ, NX, NC, NY = 8, 4, 2, 4
D = 896
TOK = 2048
ROWS = TOK // NY
HALF = ROWS // 2
QC, KC = 224, 32
PACK = 512
XC = QC + 2 * KC
WL = 1024
WX = WL // 4
RANK = 32
NB = 3
NR = NB * RANK
PIECES = NC * NX
PR = NR // PIECES
WR = XC // NC


def nt(a, b, precision=None):
    return lax.dot_general(
        a, b, (((1,), (1,)), ((), ())), precision=precision, preferred_element_type=F32
    )


def tn(a, b, precision=None):
    return lax.dot_general(
        a, b, (((0,), (0,)), ((), ())), precision=precision, preferred_element_type=F32
    )


def nn(a, b, precision=None):
    return jnp.dot(a, b, precision=precision, preferred_element_type=F32)


def split3(a):
    hi = a.astype(BF16)
    rest = a - hi.astype(F32)
    mid = rest.astype(BF16)
    low = (rest - mid.astype(F32)).astype(BF16)
    return hi, mid, low


def in_block(shape):
    row = lax.broadcasted_iota(jnp.int32, shape, 0)
    col = lax.broadcasted_iota(jnp.int32, shape, 1)
    block = (col >= QC).astype(jnp.int32) + (col >= XC).astype(jnp.int32)
    return (row // RANK) == block


def rcopy(src, dst, send, recv, dev):
    return pltpu.make_async_remote_copy(
        src_ref=src, dst_ref=dst, send_sem=send, recv_sem=recv, device_id=dev, device_id_type=MESH
    )


def inverse_factor(gram):
    row = lax.broadcasted_iota(jnp.int32, (RANK, RANK), 0)
    col = lax.broadcasted_iota(jnp.int32, (RANK, RANK), 1)
    eye = (row == col).astype(F32)
    work = jnp.concatenate([eye, gram], axis=1)
    sub = lax.broadcasted_iota(jnp.int32, (RANK, 2 * RANK), 0)
    for k in range(RANK):
        pivot = work[k : k + 1, RANK + k : RANK + k + 1]
        inv = 1.0 / jnp.sqrt(pivot)
        row_k = work[k : k + 1, :] * inv
        col_k = work[:, RANK + k : RANK + k + 1] * inv
        work = jnp.where(sub > k, work - col_k * row_k, jnp.where(sub == k, row_k, work))
    return work[:, :RANK]


def body(
    X, DQ, DK, DV, CX, DO, WQ, WK, WV, WO, ER, FI,
    GI, GC, NE, CG,
    xg, og, cot, wo, er, fi, wf, qf, acc,
    pts, ptr, lts, rcore, s1, rx, sz, rz, sy, ry, gl, lt, bas,
    rt, rcr, q1, rxr, q2, rzr, gr, rtot,
    giv, gcv, nev, cgv,
    ld, st, ag_s, ag_r, fw_s, fw_r, p_s, p_r, c_s, c_r, x_s, x_r, z_s, z_r, w_s, w_r, y_s, y_r, q_s, q_r,
):
    d = lax.axis_index("dp")
    y = lax.axis_index("tensor")
    z, x, c = d // (NX * NC), (d // NC) % NX, d % NC

    def dev(z_, x_, c_, y_):
        return ((z_ * NX + x_) * NC + c_, y_)

    core_dev = dev(z, x, 1 - c, y)
    x_dev = [dev(z, (x + k) % NX, c, y) for k in range(NX)]
    z_dev = [dev((z + k) % NZ, x, c, y) for k in range(NZ)]
    y_dev = [dev(z, x, c, (y + k) % NY) for k in range(NY)]

    def start(copies):
        for cp in copies:
            cp.start()

    def wait(copies):
        for cp in copies:
            cp.wait()

    barrier = pltpu.get_barrier_semaphore()
    peers = [core_dev] + x_dev[1:] + z_dev[1:] + y_dev[1:]
    for p in peers:
        pl.semaphore_signal(barrier, inc=1, device_id=p, device_id_type=MESH)

    pairs = [
        (WQ, wf.at[0, 0:QC, 0:D]), (WK, wf.at[0, QC : QC + KC, 0:D]), (WV, wf.at[0, QC + KC : XC, 0:D]),
        (DQ, cot.at[0:QC]), (DK, cot.at[QC : QC + KC]), (DV, cot.at[QC + KC : XC]), (CX, cot.at[XC:PACK]),
        (FI, fi), (ER, er), (X, xg.at[0]), (DO, og.at[0]), (WO, wo),
    ]
    loads = [pltpu.make_async_copy(a, b, ld.at[i]) for i, (a, b) in enumerate(pairs)]
    start(loads)
    wf[0, :, D:] = jnp.zeros((XC, WL - D), BF16)
    wait(loads[:3])
    pl.semaphore_wait(barrier, len(peers))

    wrows, wcols = pl.ds(pl.multiple_of(c * WR, 16), WR), pl.ds(pl.multiple_of(x * WX, 128), WX)
    w_y = [rcopy(wf.at[0, wrows, wcols], wf.at[k, wrows, wcols], y_s.at[1, k], y_r.at[1, k], y_dev[NY - k])
           for k in range(1, NY)]
    start(w_y)

    wait(loads[3:8])
    fm = jnp.where(in_block((NR, PACK)), jnp.concatenate([fi[...]] * NB, axis=0), 0.0)
    fm3 = jnp.concatenate(split3(fm), axis=0)

    def token_cols(k):
        return pl.ds(pl.multiple_of(((y + NY - k) % NY) * ROWS, ROWS), ROWS)

    for k in (1, 3, 2, 0):
        prod = nn(fm3, cot[:, token_cols(k)])
        dst = ptr if k == 0 else pts
        dst[k] = prod[:NR] + prod[NR : 2 * NR] + prod[2 * NR :]
    p_y = [rcopy(pts.at[k], ptr.at[k], p_s.at[k], p_r.at[k], y_dev[NY - k]) for k in (1, 3, 2)]
    start(p_y)

    def own_sends(i, src, dst):
        out = []
        for n in range(2):
            for way in (1, 3):
                h = n if way == 1 else 1 - n
                rows = pl.ds(h * HALF, HALF)
                out.append(rcopy(src.at[rows], dst.at[way, rows],
                                 ag_s.at[i, way, h], ag_r.at[i, way, h], y_dev[way]))
        return out

    def forwards(i, buf):
        out = []
        for h, way in ((0, 1), (1, 3)):
            rows = pl.ds(h * HALF, HALF)
            out.append(rcopy(buf.at[way, rows], buf.at[2, rows], fw_s.at[i, h], fw_r.at[i, h], y_dev[way]))
        return out

    own_o, own_x = own_sends(0, DO, og), own_sends(1, X, xg)
    fwd_o, fwd_x = forwards(0, og), forwards(1, xg)
    start(own_o)
    start(own_x)

    wait(w_y)
    w_x = [rcopy(wf.at[pl.ds(1, NY - 1), wrows, wcols], wf.at[pl.ds(1, NY - 1), wrows, wcols],
                 w_s.at[k], w_r.at[k], x_dev[k]) for k in range(1, NX)]
    start(w_x)

    def grads_x(slot):
        acc[0:XC, :] += nn(cot[0:XC, token_cols(slot)], xg[slot])

    def grads_o(slot):
        acc[XC:PACK, :] += nn(cot[XC:PACK, token_cols(slot)], og[slot])

    def contexts(slot):
        gcv[:, token_cols(slot)] = nt(wo[...], og[slot]).astype(BF16)

    scale = float(TOK) ** (-0.5)
    wait(loads[8:])
    own_e = nt(fm, er[...], PRECISE)
    acc[...] = er[...].T * (float(TOK) ** 0.5)
    grads_x(0)
    grads_o(0)
    contexts(0)

    wait(p_y)
    for k in range(NY):
        parts = split3(ptr[k])
        up = nn(jnp.concatenate([t[: 2 * RANK] for t in parts], axis=0), xg[0])
        lo = nn(jnp.concatenate([t[2 * RANK :] for t in parts], axis=0), og[0])
        up = up[: 2 * RANK] + up[2 * RANK : 4 * RANK] + up[4 * RANK :]
        lo = lo[:RANK] + lo[RANK : 2 * RANK] + lo[2 * RANK :]
        left = jnp.concatenate([up, lo], axis=0) * scale
        if k == 0:
            left = left + own_e
        for p in range(PIECES):
            lts[p, k * PR : (k + 1) * PR, :] = left[p * PR : (p + 1) * PR, :]

    lc = rcopy(lts.at[pl.ds(NX * (1 - c), NX)], rcore, c_s.at[0], c_r.at[0], core_dev)
    lc.start()
    wait(w_x)
    w_c = rcopy(wf.at[pl.ds(1, NY - 1), wrows], wf.at[pl.ds(1, NY - 1), wrows], c_s.at[4], c_r.at[4], core_dev)
    lc.wait()
    w_c.start()
    s1[...] = lts[pl.ds(NX * c, NX)] + rcore[...]
    lx = [rcopy(s1.at[(x + k) % NX], rx.at[k], x_s.at[0, k], x_r.at[0, k], x_dev[k]) for k in range(1, NX)]
    start(lx)
    wait(lx)
    s2 = s1[x] + rx[1] + rx[2] + rx[3]
    for i in range(NZ - 1):
        sz[i] = s2[:, i * 128 : (i + 1) * 128]
    sz[NZ - 1] = jnp.zeros_like(sz[NZ - 1])
    lz = [rcopy(sz.at[(z + k) % NZ], rz.at[k], z_s.at[0, k], z_r.at[0, k], z_dev[k]) for k in range(1, NZ)]
    start(lz)
    wait(lz)
    s3 = sz[z]
    for k in range(1, NZ):
        s3 = s3 + rz[k]
    sy[...] = jnp.zeros_like(sy)
    for k in range(NY):
        sy[k, 0:PR, :] = s3[k * PR : (k + 1) * PR, :]
    ly = [rcopy(sy.at[k], ry.at[k], y_s.at[0, k], y_r.at[0, k], y_dev[k]) for k in range(1, NY)]
    start(ly)
    wait(own_o)
    start(fwd_o)
    for slot in (1, 3):
        grads_o(slot)
        contexts(slot)
    wait(ly)
    gl[c, x, z] = sy[0] + ry[1] + ry[2] + ry[3]
    gz = [rcopy(gl.at[c, x, z], gl.at[c, x, z], z_s.at[1, k], z_r.at[1, k], z_dev[k]) for k in range(1, NZ)]
    start(gz)
    wait(own_x)
    start(fwd_x)
    q_y = [rcopy(cot.at[0:XC, token_cols(k)], qf.at[k], q_s.at[k], q_r.at[k], y_dev[NY - k]) for k in (1, 3, 2)]
    start(q_y)
    wait(gz)
    gx = [rcopy(gl.at[c, x], gl.at[c, x], x_s.at[1, k], x_r.at[1, k], x_dev[k]) for k in range(1, NX)]
    start(gx)
    grads_x(1)
    wait(gx)
    gc = rcopy(gl.at[c], gl.at[c], c_s.at[1], c_r.at[1], core_dev)
    gc.start()
    grads_x(3)
    gc.wait()
    for p in range(PIECES):
        for i in range(NZ - 1):
            lt[p * PR : (p + 1) * PR, i * 128 : (i + 1) * 128] = gl[p // NX, p % NX, i, 0:PR, :]
    for b in range(NB):
        left = lt[b * RANK : (b + 1) * RANK, :]
        bas[b * RANK : (b + 1) * RANK, :] = nn(inverse_factor(nt(left, left, PRECISE)), left, PRECISE)

    wait(fwd_o)
    grads_o(2)
    contexts(2)
    out_gc = pltpu.make_async_copy(gcv, GC, st.at[1])
    out_gc.start()
    wait(fwd_x)
    grads_x(2)
    acc[...] = acc[...] * scale

    right = jnp.where(in_block((NR, PACK)), nt(bas[...], acc[...], PRECISE), 0.0)
    rt[...] = right[:RANK] + right[RANK : 2 * RANK] + right[2 * RANK :]
    hr = RANK // NC
    rc = rcopy(rt.at[pl.ds(pl.multiple_of((1 - c) * hr, 8), hr)], rcr, c_s.at[2], c_r.at[2], core_dev)
    rc.start()
    rc.wait()
    s = rt[pl.ds(pl.multiple_of(c * hr, 8), hr), :] + rcr[...]
    for i in range(NX):
        q1[i] = s[:, i * 128 : (i + 1) * 128]
    rxs = [rcopy(q1.at[(x + k) % NX], rxr.at[k], x_s.at[2, k], x_r.at[2, k], x_dev[k]) for k in range(1, NX)]
    start(rxs)
    wait(rxs)
    q2[...] = q1[x] + rxr[1] + rxr[2] + rxr[3]
    rzs = [rcopy(q2, rzr.at[k], z_s.at[2, k], z_r.at[2, k], z_dev[k]) for k in range(1, NZ)]
    start(rzs)
    nev[...] = acc[...].T - tn(bas[...], right, PRECISE)
    out_ne = pltpu.make_async_copy(nev, NE, st.at[2])
    out_ne.start()
    wait(rzs)
    rzr[0] = q2[...]
    total = rzr[z % NZ]
    for i in range(1, NZ):
        total = total + rzr[(z + NZ - i) % NZ]
    gr[c, x] = total
    rxg = [rcopy(gr.at[c, x], gr.at[c, x], x_s.at[3, k], x_r.at[3, k], x_dev[k]) for k in range(1, NX)]
    start(rxg)
    wait(rxg)
    rcg = rcopy(gr.at[c], gr.at[c], c_s.at[3], c_r.at[3], core_dev)
    rcg.start()
    rcg.wait()
    for p in range(NC):
        for i in range(NX):
            rtot[p * hr : (p + 1) * hr, i * 128 : (i + 1) * 128] = gr[p, i]
    full = jnp.where(in_block((NR, PACK)), jnp.concatenate([rtot[...]] * NB, axis=0), 0.0)
    cgv[...] = tn(bas[...], full, PRECISE)
    out_cg = pltpu.make_async_copy(cgv, CG, st.at[3])
    out_cg.start()

    w_c.wait()
    wait(q_y)
    out = tn(cot[0:XC, token_cols(0)], wf[0, :, 0:D])
    for k in range(1, NY):
        out = out + tn(qf[k], wf[k, :, 0:D])
    giv[...] = out.astype(BF16)
    out_gi = pltpu.make_async_copy(giv, GI, st.at[0])
    out_gi.start()
    wait((out_gc, out_ne, out_cg, out_gi))


def on_device(
    normed_input, grad_query, grad_key, grad_value, context, grad_output,
    w_query, w_key, w_value, w_output, error, factor_init,
):
    any_spec = pl.BlockSpec(memory_space=pl.ANY)
    V = pltpu.VMEM
    hr = RANK // NC
    scratch = [
        V((NY, ROWS, D), BF16), V((NY, ROWS, D), BF16), V((PACK, TOK), BF16),
        V((QC, D), BF16), V((D, PACK), F32), V((RANK, PACK), F32),
        V((NY, XC, WL), BF16), V((NY, XC, ROWS), BF16), V((PACK, D), F32),
        V((NY, NR, ROWS), F32), V((NY, NR, ROWS), F32),
        V((PIECES, NY * PR, D), F32), V((NX, NY * PR, D), F32), V((NX, NY * PR, D), F32),
        V((NX, NY * PR, D), F32), V((NZ, NY * PR, 128), F32), V((NZ, NY * PR, 128), F32),
        V((NY, 16, 128), F32), V((NY, 16, 128), F32), V((NC, NX, NZ, 16, 128), F32),
        V((NR, D), F32), V((NR, D), F32),
        V((RANK, PACK), F32), V((hr, PACK), F32), V((NX, hr, 128), F32), V((NX, hr, 128), F32),
        V((hr, 128), F32), V((NZ, hr, 128), F32), V((NC, NX, hr, 128), F32), V((RANK, PACK), F32),
        V((ROWS, D), BF16), V((QC, TOK), BF16), V((D, PACK), F32), V((D, PACK), F32),
    ]
    S = pltpu.SemaphoreType.DMA
    sems = [
        S((12,)), S((4,)), S((2, 4, 2)), S((2, 4, 2)), S((2, 2)), S((2, 2)), S((NY,)), S((NY,)),
        S((5,)), S((5,)), S((4, NX)), S((4, NX)), S((3, NZ)), S((3, NZ)),
        S((NX,)), S((NX,)), S((2, NY)), S((2, NY)), S((NY,)), S((NY,)),
    ]
    grad_input, grad_context, new_error, compressed = pl.pallas_call(
        body,
        out_shape=(
            jax.ShapeDtypeStruct((ROWS, D), BF16),
            jax.ShapeDtypeStruct((QC, TOK), BF16),
            jax.ShapeDtypeStruct((D, PACK), F32),
            jax.ShapeDtypeStruct((D, PACK), F32),
        ),
        in_specs=[any_spec] * 12,
        out_specs=(any_spec,) * 4,
        scratch_shapes=scratch + sems,
        compiler_params=pltpu.CompilerParams(
            collective_id=0, has_side_effects=True, vmem_limit_bytes=60 * 2**20
        ),
        name="backward",
    )(
        normed_input, grad_query.T, grad_key.T, grad_value.T, context.T, grad_output,
        w_query.T, w_key.T, w_value.T, w_output, error, factor_init.T,
    )
    return grad_input, grad_context.T, new_error, compressed


def solution(mesh):
    return jax.shard_map(
        on_device,
        mesh=mesh,
        in_specs=(
            P(("dp", "tensor"), None),
            P("dp", "tensor"),
            P("dp", "tensor"),
            P("dp", "tensor"),
            P("dp", "tensor"),
            P(("dp", "tensor"), None),
            P(None, "tensor"),
            P(None, "tensor"),
            P(None, "tensor"),
            P("tensor", None),
            P("dp", "tensor"),
            P("tensor", None),
        ),
        out_specs=(
            P(("dp", "tensor"), None),
            P("dp", "tensor"),
            P("dp", "tensor"),
            P(None, "tensor"),
        ),
        check_vma=False,
    )
```

```python
import jax
import jax.numpy as jnp
from jax import lax
from jax.experimental import pallas as pl
from jax.experimental.pallas import tpu as pltpu
from jax.sharding import PartitionSpec as P

MESH = pl.DeviceIdType.MESH
F32, BF16 = jnp.float32, jnp.bfloat16
PRECISE = lax.Precision.HIGHEST
NZ, NX, NC, NY = 8, 4, 2, 4
D = 896
TOK = 2048
ROWS = TOK // NY
CH = 4
CHR = ROWS // CH
QC, KC = 224, 32
PACK = 512
XC = QC + 2 * KC
WL = 1024
WX = WL // 4
RANK = 32
NB = 3
NR = NB * RANK
PIECES = NC * NX
PR = NR // PIECES
WR = XC // NC


def nt(a, b, precision=None):
    return lax.dot_general(
        a, b, (((1,), (1,)), ((), ())), precision=precision, preferred_element_type=F32
    )


def tn(a, b, precision=None):
    return lax.dot_general(
        a, b, (((0,), (0,)), ((), ())), precision=precision, preferred_element_type=F32
    )


def nn(a, b, precision=None):
    return jnp.dot(a, b, precision=precision, preferred_element_type=F32)


def split3(a):
    hi = a.astype(BF16)
    rest = a - hi.astype(F32)
    mid = rest.astype(BF16)
    low = (rest - mid.astype(F32)).astype(BF16)
    return hi, mid, low


def in_block(shape):
    row = lax.broadcasted_iota(jnp.int32, shape, 0)
    col = lax.broadcasted_iota(jnp.int32, shape, 1)
    block = (col >= QC).astype(jnp.int32) + (col >= XC).astype(jnp.int32)
    return (row // RANK) == block


def rcopy(src, dst, send, recv, dev):
    return pltpu.make_async_remote_copy(
        src_ref=src, dst_ref=dst, send_sem=send, recv_sem=recv, device_id=dev, device_id_type=MESH
    )


def inverse_factor(gram):
    row = lax.broadcasted_iota(jnp.int32, (RANK, RANK), 0)
    col = lax.broadcasted_iota(jnp.int32, (RANK, RANK), 1)
    eye = (row == col).astype(F32)
    work = jnp.concatenate([eye, gram], axis=1)
    sub = lax.broadcasted_iota(jnp.int32, (RANK, 2 * RANK), 0)
    for k in range(RANK):
        pivot = work[k : k + 1, RANK + k : RANK + k + 1]
        inv = 1.0 / jnp.sqrt(pivot)
        row_k = work[k : k + 1, :] * inv
        col_k = work[:, RANK + k : RANK + k + 1] * inv
        work = jnp.where(sub > k, work - col_k * row_k, jnp.where(sub == k, row_k, work))
    return work[:, :RANK]


def body(
    X, DQ, DK, DV, CX, DO, WQ, WK, WV, WO, ER, FI,
    GI, GC, NE, BA, GR,
    xg, og, cot, wo, er, fi, wf, qf, acc,
    pts, ptr, lts, rcore, s1, rx, sz, rz, sy, ry, gl, lt, bas,
    rpart, q1, rxr, q2, rzr, gr,
    giv, gcv, nev, bav,
    ld, st, ag_s, ag_r, fw_s, fw_r, p_s, p_r, c_s, c_r, x_s, x_r, z_s, z_r, w_s, w_r, y_s, y_r, q_s, q_r, r_s, r_r,
):
    d = lax.axis_index("dp")
    y = lax.axis_index("tensor")
    z, x, c = d // (NX * NC), (d // NC) % NX, d % NC

    def dev(z_, x_, c_, y_):
        return ((z_ * NX + x_) * NC + c_, y_)

    core_dev = dev(z, x, 1 - c, y)
    x_dev = [dev(z, (x + k) % NX, c, y) for k in range(NX)]
    z_dev = [dev((z + k) % NZ, x, c, y) for k in range(NZ)]
    y_dev = [dev(z, x, c, (y + k) % NY) for k in range(NY)]
    row = [(e, k) for k in range(NX) for e in range(NC)][1:]
    row_dev = {(e, k): dev(z, (x + k) % NX, (c + e) % NC, y) for e, k in row}

    def start(copies):
        for cp in copies:
            cp.start()

    def wait(copies):
        for cp in copies:
            cp.wait()

    barrier = pltpu.get_barrier_semaphore()
    peers = list(row_dev.values()) + z_dev[1:] + y_dev[1:]
    for p in peers:
        pl.semaphore_signal(barrier, inc=1, device_id=p, device_id_type=MESH)

    pairs = [
        (WQ, wf.at[0, 0:QC, 0:D]), (WK, wf.at[0, QC : QC + KC, 0:D]), (WV, wf.at[0, QC + KC : XC, 0:D]),
        (DQ, cot.at[0:QC]), (DK, cot.at[QC : QC + KC]), (DV, cot.at[QC + KC : XC]), (CX, cot.at[XC:PACK]),
        (FI, fi), (ER, er), (X, xg.at[0]), (DO, og.at[0]), (WO, wo),
    ]
    loads = [pltpu.make_async_copy(a, b, ld.at[i]) for i, (a, b) in enumerate(pairs)]
    start(loads)
    wf[0, :, D:] = jnp.zeros((XC, WL - D), BF16)
    pl.semaphore_wait(barrier, len(peers))

    def own_sends(i, src, dst):
        out = []
        for n in range(CH):
            for way, h in ((1, n), (3, CH - 1 - n)):
                rows = pl.ds(h * CHR, CHR)
                out.append(rcopy(src.at[rows], dst.at[way, rows],
                                 ag_s.at[i, way, h], ag_r.at[i, way, h], y_dev[way]))
        return out

    def forwards(i, buf):
        out = []
        for n in range(CH // 2):
            for way, h in ((1, n), (3, CH - 1 - n)):
                rows = pl.ds(h * CHR, CHR)
                out.append(rcopy(buf.at[way, rows], buf.at[2, rows], fw_s.at[i, h], fw_r.at[i, h], y_dev[way]))
        return out

    own_o, own_x = own_sends(0, DO, og), own_sends(1, X, xg)
    fwd_o, fwd_x = forwards(0, og), forwards(1, xg)
    start(own_o[:2])

    wrows, wcols = pl.ds(pl.multiple_of(c * WR, 16), WR), pl.ds(pl.multiple_of(x * WX, 128), WX)
    w_y = [rcopy(wf.at[0, wrows, wcols], wf.at[k, wrows, wcols], y_s.at[1, k], y_r.at[1, k], y_dev[NY - k])
           for k in range(1, NY)]
    wait(loads[:3])
    start(w_y)

    wait(loads[3:8])
    fm = jnp.where(in_block((NR, PACK)), jnp.concatenate([fi[...]] * NB, axis=0), 0.0)
    fm3 = jnp.concatenate(split3(fm), axis=0)

    def token_cols(k):
        return pl.ds(pl.multiple_of(((y + NY - k) % NY) * ROWS, ROWS), ROWS)

    for k in (1, 3, 2, 0):
        prod = nn(fm3, cot[:, token_cols(k)])
        dst = ptr if k == 0 else pts
        dst[k] = prod[:NR] + prod[NR : 2 * NR] + prod[2 * NR :]
    p_y = [rcopy(pts.at[k], ptr.at[k], p_s.at[k], p_r.at[k], y_dev[NY - k]) for k in (1, 3, 2)]
    start(p_y)

    start(own_o[2:])
    start(own_x[:2])

    wait(w_y)
    w_x = [rcopy(wf.at[pl.ds(1, NY - 1), wrows, wcols], wf.at[pl.ds(1, NY - 1), wrows, wcols],
                 w_s.at[k], w_r.at[k], x_dev[k]) for k in range(1, NX)]
    start(w_x)

    def grads_x(slot):
        acc[0:XC, :] += nn(cot[0:XC, token_cols(slot)], xg[slot])

    def grads_o(slot):
        acc[XC:PACK, :] += nn(cot[XC:PACK, token_cols(slot)], og[slot])

    def contexts(slot):
        gcv[:, token_cols(slot)] = nt(wo[...], og[slot]).astype(BF16)

    scale = float(TOK) ** (-0.5)
    wait(loads[8:])
    own_e = nt(fm, er[...], PRECISE)
    acc[...] = er[...].T * (float(TOK) ** 0.5)
    grads_x(0)
    grads_o(0)
    contexts(0)

    def left_from(k):
        parts = split3(ptr[k])
        up = nn(jnp.concatenate([t[: 2 * RANK] for t in parts], axis=0), xg[0])
        lo = nn(jnp.concatenate([t[2 * RANK :] for t in parts], axis=0), og[0])
        up = up[: 2 * RANK] + up[2 * RANK : 4 * RANK] + up[4 * RANK :]
        lo = lo[:RANK] + lo[RANK : 2 * RANK] + lo[2 * RANK :]
        left = jnp.concatenate([up, lo], axis=0) * scale
        if k == 0:
            left = left + own_e
        for p in range(PIECES):
            lts[p, k * PR : (k + 1) * PR, :] = left[p * PR : (p + 1) * PR, :]

    left_from(0)
    for cp, k in zip(p_y, (1, 3, 2)):
        cp.wait()
        left_from(k)

    lc = rcopy(lts.at[pl.ds(NX * (1 - c), NX)], rcore, c_s.at[0], c_r.at[0], core_dev)
    lc.start()
    wait(w_x)
    w_c = rcopy(wf.at[pl.ds(1, NY - 1), wrows], wf.at[pl.ds(1, NY - 1), wrows], c_s.at[4], c_r.at[4], core_dev)
    lc.wait()
    w_c.start()
    s1[...] = lts[pl.ds(NX * c, NX)] + rcore[...]
    lx = [rcopy(s1.at[(x + k) % NX], rx.at[k], x_s.at[0, k], x_r.at[0, k], x_dev[k]) for k in range(1, NX)]
    start(lx)
    wait(own_o)
    grads_o(1)
    contexts(1)
    wait(lx)
    start(own_x[2:4])
    s2 = s1[x] + rx[1] + rx[2] + rx[3]
    for i in range(NZ - 1):
        sz[i] = s2[:, i * 128 : (i + 1) * 128]
    sz[NZ - 1] = jnp.zeros_like(sz[NZ - 1])
    lz = [rcopy(sz.at[(z + k) % NZ], rz.at[k], z_s.at[0, k], z_r.at[0, k], z_dev[k]) for k in range(1, NZ)]
    start(lz)
    wait(lz)
    s3 = sz[z]
    for k in range(1, NZ):
        s3 = s3 + rz[k]
    sy[...] = jnp.zeros_like(sy)
    for k in range(NY):
        sy[k, 0:PR, :] = s3[k * PR : (k + 1) * PR, :]
    ly = [rcopy(sy.at[k], ry.at[k], y_s.at[0, k], y_r.at[0, k], y_dev[k]) for k in range(1, NY)]
    start(ly)
    start(own_x[4:])
    start(fwd_o)
    wait(ly)
    gl[c, x, z] = sy[0] + ry[1] + ry[2] + ry[3]
    gz = [rcopy(gl.at[c, x, z], gl.at[c, x, z], z_s.at[1, k], z_r.at[1, k], z_dev[k]) for k in range(1, NZ)]
    start(gz)
    grads_o(3)
    wait(gz)
    gx = [rcopy(gl.at[c, x], gl.at[c, x], x_s.at[1, k], x_r.at[1, k], x_dev[k]) for k in range(1, NX)]
    start(gx)
    contexts(3)
    wait(gx)
    gc = rcopy(gl.at[c], gl.at[c], c_s.at[1], c_r.at[1], core_dev)
    gc.start()
    wait(own_x)
    start(fwd_x)
    q_y = [rcopy(cot.at[0:XC, token_cols(k)], qf.at[k], q_s.at[k], q_r.at[k], y_dev[NY - k]) for k in (1, 3, 2)]
    start(q_y)
    gc.wait()
    for p in range(PIECES):
        for i in range(NZ - 1):
            lt[p * PR : (p + 1) * PR, i * 128 : (i + 1) * 128] = gl[p // NX, p % NX, i, 0:PR, :]
    for b in range(NB):
        left = lt[b * RANK : (b + 1) * RANK, :]
        bas[b * RANK : (b + 1) * RANK, :] = nn(inverse_factor(nt(left, left, PRECISE)), left, PRECISE)

    grads_x(1)
    grads_x(3)
    qf[0] = cot[0:XC, token_cols(0)]
    for i in range(2):
        hi, mid, _ = split3(bas[i * RANK : (i + 2) * RANK, :])
        terms = jnp.concatenate([hi, hi, mid, mid], axis=0).astype(F32)
        bav[i] = terms.T.astype(BF16)
    out_ba = pltpu.make_async_copy(bav, BA, st.at[3])
    out_ba.start()
    wait(fwd_o)
    grads_o(2)
    contexts(2)
    out_gc = pltpu.make_async_copy(gcv, GC, st.at[1])
    out_gc.start()

    rpart[...] = nt(bas[...], acc[...], PRECISE)
    bas3 = jnp.concatenate(split3(bas[...]), axis=0)
    wait(fwd_x)
    last = nt(bas3, xg[2])
    last = jnp.concatenate(split3(last[:NR] + last[NR : 2 * NR] + last[2 * NR :]), axis=0)
    last = nt(last, cot[0:XC, token_cols(2)])
    rpart[:, 0:XC] += last[:NR] + last[NR : 2 * NR] + last[2 * NR :]
    right = jnp.where(in_block((NR, PACK)), rpart[...] * scale, 0.0)
    packed = right[:RANK] + right[RANK : 2 * RANK] + right[2 * RANK :]
    hr = RANK // NC
    for e in range(NC):
        for i in range(NX):
            q1[e, i] = packed[e * hr : (e + 1) * hr, i * 128 : (i + 1) * 128]
    r1 = [rcopy(q1.at[(c + e) % NC, (x + k) % NX], rxr.at[e, k], r_s.at[0, e, k], r_r.at[0, e, k], row_dev[e, k])
          for e, k in row]
    start(r1)
    grads_x(2)
    wait(r1)
    mine = q1[c, x]
    for e, k in row:
        mine = mine + rxr[e, k]
    q2[...] = mine
    r2 = [rcopy(q2, rzr.at[k], z_s.at[2, k], z_r.at[2, k], z_dev[k]) for k in range(1, NZ)]
    start(r2)
    nev[...] = acc[...].T * scale - tn(bas[...], right, PRECISE)
    out_ne = pltpu.make_async_copy(nev, NE, st.at[2])
    out_ne.start()
    wait(r2)
    rzr[0] = q2[...]
    total = rzr[z % NZ]
    for i in range(1, NZ):
        total = total + rzr[(z + NZ - i) % NZ]
    gr[c, x] = total
    r3 = [rcopy(gr.at[c, x], gr.at[c, x], r_s.at[1, e, k], r_r.at[1, e, k], row_dev[e, k]) for e, k in row]
    start(r3)

    w_c.wait()
    wait(q_y)
    giv[...] = tn(qf[...].reshape(NY * XC, ROWS), wf[...].reshape(NY * XC, WL)[:, :D]).astype(BF16)
    out_gi = pltpu.make_async_copy(giv, GI, st.at[0])
    out_gi.start()
    wait(r3)
    out_gr = pltpu.make_async_copy(gr, GR, st.at[4])
    out_gr.start()
    wait((out_gc, out_ne, out_ba, out_gi, out_gr))


def finish(GI, GC, NE, BA, GR, gi_out, gc_out, ne_out, cg_out, gi, gc, ne, ba, gr, cg, sem):
    loads = [
        pltpu.make_async_copy(a, b, sem.at[i])
        for i, (a, b) in enumerate(((GR, gr), (BA, ba), (NE, ne), (GI, gi), (GC, gc)))
    ]
    for cp in loads:
        cp.start()
    loads[0].wait()
    hr = RANK // NC
    col = lax.broadcasted_iota(jnp.int32, (RANK, 256), 1)
    rhs = []
    for i, edge in ((0, QC), (1, XC - 256)):
        total = jnp.concatenate(
            [jnp.concatenate([gr[e, 2 * i], gr[e, 2 * i + 1]], axis=1) for e in range(NC)], axis=0
        )
        total = jnp.concatenate([jnp.where(col < edge, total, 0.0), jnp.where(col < edge, 0.0, total)], axis=0)
        hi, mid, _ = split3(total)
        rhs.append(jnp.concatenate([hi, mid, hi, mid], axis=0))
    loads[1].wait()
    stores = []

    def store(src, dst):
        cp = pltpu.make_async_copy(src, dst, sem.at[5 + len(stores)])
        cp.start()
        stores.append(cp)

    half = D // 2
    for r in range(2):
        rows = pl.ds(r * half, half)
        for i in range(2):
            cg[rows, i * 256 : (i + 1) * 256] = nn(ba[i, rows, :], rhs[i])
        store(cg.at[rows], cg_out.at[rows])
    for cp, src, dst in zip(loads[2:], (ne, gi, gc), (ne_out, gi_out, gc_out)):
        cp.wait()
        store(src, dst)
    for cp in stores:
        cp.wait()


def on_device(
    normed_input, grad_query, grad_key, grad_value, context, grad_output,
    w_query, w_key, w_value, w_output, error, factor_init,
):
    any_spec = pl.BlockSpec(memory_space=pl.ANY)
    V = pltpu.VMEM
    hr = RANK // NC
    scratch = [
        V((NY, ROWS, D), BF16), V((NY, ROWS, D), BF16), V((PACK, TOK), BF16),
        V((QC, D), BF16), V((D, PACK), F32), V((RANK, PACK), F32),
        V((NY, XC, WL), BF16), V((NY, XC, ROWS), BF16), V((PACK, D), F32),
        V((NY, NR, ROWS), F32), V((NY, NR, ROWS), F32),
        V((PIECES, NY * PR, D), F32), V((NX, NY * PR, D), F32), V((NX, NY * PR, D), F32),
        V((NX, NY * PR, D), F32), V((NZ, NY * PR, 128), F32), V((NZ, NY * PR, 128), F32),
        V((NY, 16, 128), F32), V((NY, 16, 128), F32), V((NC, NX, NZ, 16, 128), F32),
        V((NR, D), F32), V((NR, D), F32),
        V((NR, PACK), F32), V((NC, NX, hr, 128), F32), V((NC, NX, hr, 128), F32),
        V((hr, 128), F32), V((NZ, hr, 128), F32), V((NC, NX, hr, 128), F32),
        V((ROWS, D), BF16), V((QC, TOK), BF16), V((D, PACK), F32), V((2, D, 256), BF16),
    ]
    S = pltpu.SemaphoreType.DMA
    sems = [
        S((12,)), S((5,)), S((2, 4, CH)), S((2, 4, CH)), S((2, CH)), S((2, CH)), S((NY,)), S((NY,)),
        S((5,)), S((5,)), S((4, NX)), S((4, NX)), S((3, NZ)), S((3, NZ)),
        S((NX,)), S((NX,)), S((2, NY)), S((2, NY)), S((NY,)), S((NY,)),
        S((2, NC, NX)), S((2, NC, NX)),
    ]
    outs = (
        jax.ShapeDtypeStruct((ROWS, D), BF16),
        jax.ShapeDtypeStruct((QC, TOK), BF16),
        jax.ShapeDtypeStruct((D, PACK), F32),
    )
    parts = pl.pallas_call(
        body,
        out_shape=outs[:3] + (
            jax.ShapeDtypeStruct((2, D, 256), BF16),
            jax.ShapeDtypeStruct((NC, NX, hr, 128), F32),
        ),
        in_specs=[any_spec] * 12,
        out_specs=(any_spec,) * 5,
        scratch_shapes=scratch + sems,
        compiler_params=pltpu.CompilerParams(
            collective_id=0, has_side_effects=True, vmem_limit_bytes=60 * 2**20
        ),
        name="backward",
    )(
        normed_input, grad_query.T, grad_key.T, grad_value.T, context.T, grad_output,
        w_query.T, w_key.T, w_value.T, w_output, error, factor_init.T,
    )
    grad_input, grad_context, new_error, compressed = pl.pallas_call(
        finish,
        out_shape=outs + (jax.ShapeDtypeStruct((D, PACK), F32),),
        in_specs=[any_spec] * 5,
        out_specs=(any_spec,) * 4,
        scratch_shapes=[
            V((ROWS, D), BF16), V((QC, TOK), BF16), V((D, PACK), F32),
            V((2, D, 256), BF16), V((NC, NX, hr, 128), F32), V((D, PACK), F32), S((10,)),
        ],
        compiler_params=pltpu.CompilerParams(vmem_limit_bytes=60 * 2**20),
        name="finish",
    )(*parts)
    return grad_input, grad_context.T, new_error, compressed


def solution(mesh):
    return jax.shard_map(
        on_device,
        mesh=mesh,
        in_specs=(
            P(("dp", "tensor"), None),
            P("dp", "tensor"),
            P("dp", "tensor"),
            P("dp", "tensor"),
            P("dp", "tensor"),
            P(("dp", "tensor"), None),
            P(None, "tensor"),
            P(None, "tensor"),
            P(None, "tensor"),
            P("tensor", None),
            P("dp", "tensor"),
            P("tensor", None),
        ),
        out_specs=(
            P(("dp", "tensor"), None),
            P("dp", "tensor"),
            P("dp", "tensor"),
            P(None, "tensor"),
        ),
        check_vma=False,
    )
```

```python
import jax
import jax.numpy as jnp
from jax import lax
from jax.experimental import pallas as pl
from jax.experimental.pallas import tpu as pltpu
from jax.sharding import PartitionSpec as P

MESH = pl.DeviceIdType.MESH
F32, BF16 = jnp.float32, jnp.bfloat16
PRECISE = lax.Precision.HIGHEST
NZ, NX, NC, NY = 8, 4, 2, 4
D = 896
TOK = 2048
ROWS = TOK // NY
CH = 4
CHR = ROWS // CH
QC, KC = 224, 32
PACK = 512
XC = QC + 2 * KC
WL = 1024
WX = WL // NX
SLOT = (0, 1, 3, 2)
RANK = 32
NB = 3
NR = NB * RANK
PIECES = NC * NX
XR = 2 * RANK
PR = XR // PIECES
PO = RANK // PIECES
WR = XC // NC


def nt(a, b, precision=None):
    return lax.dot_general(
        a, b, (((1,), (1,)), ((), ())), precision=precision, preferred_element_type=F32
    )


def tn(a, b, precision=None):
    return lax.dot_general(
        a, b, (((0,), (0,)), ((), ())), precision=precision, preferred_element_type=F32
    )


def nn(a, b, precision=None):
    return jnp.dot(a, b, precision=precision, preferred_element_type=F32)


def split3(a):
    hi = a.astype(BF16)
    rest = a - hi.astype(F32)
    mid = rest.astype(BF16)
    low = (rest - mid.astype(F32)).astype(BF16)
    return hi, mid, low


def in_block(shape):
    row = lax.broadcasted_iota(jnp.int32, shape, 0)
    col = lax.broadcasted_iota(jnp.int32, shape, 1)
    block = (col >= QC).astype(jnp.int32) + (col >= XC).astype(jnp.int32)
    return (row // RANK) == block


def rcopy(src, dst, send, recv, dev):
    return pltpu.make_async_remote_copy(
        src_ref=src, dst_ref=dst, send_sem=send, recv_sem=recv, device_id=dev, device_id_type=MESH
    )


def inverse_factors(grams):
    row = lax.broadcasted_iota(jnp.int32, (RANK, RANK), 0)
    col = lax.broadcasted_iota(jnp.int32, (RANK, RANK), 1)
    eye = (row == col).astype(F32)
    works = [jnp.concatenate([eye, gram], axis=1) for gram in grams]
    sub = lax.broadcasted_iota(jnp.int32, (RANK, 2 * RANK), 0)
    for k in range(RANK):
        for b, work in enumerate(works):
            pivot = work[k : k + 1, RANK + k : RANK + k + 1]
            inv = 1.0 / jnp.sqrt(pivot)
            row_k = work[k : k + 1, :] * inv
            col_k = work[:, RANK + k : RANK + k + 1] * inv
            works[b] = jnp.where(sub > k, work - col_k * row_k, jnp.where(sub == k, row_k, work))
    return [work[:, :RANK] for work in works]


def body(
    X, DQ, DK, DV, CX, DO, WQ, WK, WV, WO, ER, FI,
    GI, GC, NE, BA, GR,
    xg, og, cot, wo, er, fi, wf, qf, acc,
    pts, ptr, lts, rcore, s1, rx, sz, rz, sy, ry, gl, lt, bas,
    o1, orx, oz, orz, ol,
    rpart, q1, rxr, q2, rzr, gr,
    gacc, giv, gcv, nev, bav,
    ld, st, ag_s, ag_r, fw_s, fw_r, p_s, p_r, c_s, c_r, x_s, x_r, z_s, z_r, w_s, w_r, y_s, y_r, q_s, q_r, r_s, r_r,
):
    d = lax.axis_index("dp")
    y = lax.axis_index("tensor")
    z, x, c = d // (NX * NC), (d // NC) % NX, d % NC

    def dev(z_, x_, c_, y_):
        return ((z_ * NX + x_) * NC + c_, y_)

    core_dev = dev(z, x, 1 - c, y)
    x_dev = [dev(z, (x + k) % NX, c, y) for k in range(NX)]
    z_dev = [dev((z + k) % NZ, x, c, y) for k in range(NZ)]
    y_dev = [dev(z, x, c, (y + k) % NY) for k in range(NY)]
    row = [(e, k) for k in range(NX) for e in range(NC)][1:]
    row_dev = {(e, k): dev(z, (x + k) % NX, (c + e) % NC, y) for e, k in row}

    def start(copies):
        for cp in copies:
            cp.start()

    def wait(copies):
        for cp in copies:
            cp.wait()

    barrier = pltpu.get_barrier_semaphore()
    peers = [z_dev[k] for k in (4, 3, 5, 2, 6, 1, 7)] + list(row_dev.values()) + y_dev[1:]
    for p in peers:
        pl.semaphore_signal(barrier, inc=1, device_id=p, device_id_type=MESH)

    pairs = [
        (WQ, wf.at[0, 0:QC, 0:D]), (WK, wf.at[0, QC : QC + KC, 0:D]), (WV, wf.at[0, QC + KC : XC, 0:D]),
        (DQ, cot.at[0:QC]), (DK, cot.at[QC : QC + KC]), (DV, cot.at[QC + KC : XC]), (CX, cot.at[XC:PACK]),
        (FI, fi), (ER, er), (X, xg.at[0]), (DO, og.at[0]), (WO, wo),
    ]
    loads = [pltpu.make_async_copy(a, b, ld.at[i]) for i, (a, b) in enumerate(pairs)]
    start(loads)
    wf[0, :, D:] = jnp.zeros((XC, WL - D), BF16)
    pl.semaphore_wait(barrier, len(peers))

    def own_sends(i, src, dst):
        out = []
        for n in range(CH):
            for way, h in ((1, n), (3, CH - 1 - n)):
                rows = pl.ds(h * CHR, CHR)
                out.append(rcopy(src.at[rows], dst.at[way, rows],
                                 ag_s.at[i, way, h], ag_r.at[i, way, h], y_dev[way]))
        return out

    def forwards(i, buf):
        out = []
        for n in range(CH // 2):
            for way, h in ((1, n), (3, CH - 1 - n)):
                rows = pl.ds(h * CHR, CHR)
                out.append(rcopy(buf.at[way, rows], buf.at[2, rows], fw_s.at[i, h], fw_r.at[i, h], y_dev[way]))
        return out

    own_o, own_x = own_sends(0, DO, og), own_sends(1, X, xg)
    fwd_o, fwd_x = forwards(0, og), forwards(1, xg)
    start(own_o[:2])

    wrows, wcols = pl.ds(pl.multiple_of(c * WR, 16), WR), pl.ds(pl.multiple_of(x * WX, 128), WX)
    odd = z % 2
    wtile = pl.ds(pl.multiple_of(x * WX + odd * (WX // 2), 128), WX // 2)
    w_y = [rcopy(wf.at[0, wrows, wtile], wf.at[SLOT[k], wrows, wtile], y_s.at[1, k], y_r.at[1, k], y_dev[NY - k])
           for k in range(1, NY)]
    wait(loads[:3])
    start(w_y)

    wait(loads[3:8])
    fm = jnp.where(in_block((NR, PACK)), jnp.concatenate([fi[...]] * NB, axis=0), 0.0)
    fm3 = jnp.concatenate(split3(fm[:XR, :XC]), axis=0)

    def token_cols(k):
        return pl.ds(pl.multiple_of(((y + NY - k) % NY) * ROWS, ROWS), ROWS)

    for k in (1, 3, 2, 0):
        prod = nn(fm3, cot[0:XC, token_cols(k)])
        dst = ptr if k == 0 else pts
        dst[k] = prod[:XR] + prod[XR : 2 * XR] + prod[2 * XR :]
    p_y = [rcopy(pts.at[k], ptr.at[k], p_s.at[k], p_r.at[k], y_dev[NY - k]) for k in (1, 3, 2)]
    start(p_y)

    start(own_o[2:])

    wait(w_y)
    w_z = rcopy(wf.at[pl.ds(1, NY - 1), wrows, wtile], wf.at[pl.ds(1, NY - 1), wrows, wtile],
                w_s.at[0], w_r.at[0], dev(z + 1 - 2 * odd, x, c, y))
    w_z.start()
    w_x = [rcopy(wf.at[pl.ds(1, NY - 1), wrows, wcols], wf.at[pl.ds(1, NY - 1), wrows, wcols],
                 w_s.at[k], w_r.at[k], x_dev[k]) for k in range(1, NX)]

    def grads_x(slot):
        acc[0:XC, :] += nn(cot[0:XC, token_cols(slot)], xg[slot])

    def grads_o(slot):
        acc[XC:PACK, :] += nn(cot[XC:PACK, token_cols(slot)], og[slot])

    def contexts(slot):
        gcv[:, token_cols(slot)] = nt(wo[...], og[slot]).astype(BF16)

    scale = float(TOK) ** (-0.5)
    wait(loads[8:])
    own_e = nt(fm[:XR], er[...], PRECISE)
    acc[...] = er[...].T * (float(TOK) ** 0.5)
    w_z.wait()
    start(w_x)
    grads_x(0)
    grads_o(0)
    contexts(0)

    def left_from(k):
        left = nn(jnp.concatenate(split3(ptr[k]), axis=0), xg[0])
        left = (left[:XR] + left[XR : 2 * XR] + left[2 * XR :]) * scale
        if k == 0:
            left = left + own_e
        for p in range(PIECES):
            lts[p, k * PR : (k + 1) * PR, :] = left[p * PR : (p + 1) * PR, :]

    left_from(0)
    for cp, k in zip(p_y, (1, 3, 2)):
        cp.wait()
        left_from(k)

    wait(own_o[:2])
    start(fwd_o[:2])

    lc = rcopy(lts.at[pl.ds(NX * (1 - c), NX)], rcore, c_s.at[0], c_r.at[0], core_dev)
    lc.start()
    wait(w_x)
    w_c = rcopy(wf.at[pl.ds(1, NY - 1), wrows], wf.at[pl.ds(1, NY - 1), wrows], c_s.at[4], c_r.at[4], core_dev)
    lc.wait()
    w_c.start()
    s1[...] = lts[pl.ds(NX * c, NX)] + rcore[...]
    lx = [rcopy(s1.at[(x + k) % NX], rx.at[k], x_s.at[0, k], x_r.at[0, k], x_dev[k]) for k in range(1, NX)]
    start(lx)
    wait(own_o[2:])
    start(fwd_o[2:])
    start(own_x[:2])
    grads_o(1)
    wait(lx)
    s2 = s1[x] + rx[1] + rx[2] + rx[3]
    for i in range(NZ - 1):
        sz[i] = s2[:, i * 128 : (i + 1) * 128]
    sz[NZ - 1] = jnp.zeros_like(sz[NZ - 1])
    lz = [rcopy(sz.at[(z + k) % NZ], rz.at[k], z_s.at[0, k], z_r.at[0, k], z_dev[k]) for k in range(1, NZ)]
    start(lz)
    wait(lz)
    s3 = sz[z]
    for k in range(1, NZ):
        s3 = s3 + rz[k]
    for k in range(NY):
        sy[k] = s3[k * PR : (k + 1) * PR, :]
    ly = [rcopy(sy.at[k], ry.at[k], y_s.at[0, k], y_r.at[0, k], y_dev[k]) for k in range(1, NY)]
    start(ly)
    start(own_x[2:])
    grads_o(3)
    contexts(1)

    wait(fwd_o)
    grads_o(2)
    left_o = nn(fm[XR:], acc[...], PRECISE) * scale
    for p in range(PIECES):
        o1[p // NX, p % NX, 0:PO, :] = left_o[p * PO : (p + 1) * PO, :]
        o1[p // NX, p % NX, PO:, :] = jnp.zeros((8 - PO, D), F32)
    oa = [rcopy(o1.at[(c + e) % NC, (x + k) % NX], orx.at[e, k], r_s.at[2, e, k], r_r.at[2, e, k], row_dev[e, k])
          for e, k in row]
    start(oa)
    contexts(3)
    wait(ly)
    gl[c, x, z] = sy[0] + ry[1] + ry[2] + ry[3]
    gz = [rcopy(gl.at[c, x, z], gl.at[c, x, z], z_s.at[1, k], z_r.at[1, k], z_dev[k]) for k in range(1, NZ)]
    start(gz)
    wait(oa)
    o2 = o1[c, x]
    for e, k in row:
        o2 = o2 + orx[e, k]
    for i in range(NZ - 1):
        oz[i] = o2[:, i * 128 : (i + 1) * 128]
    oz[NZ - 1] = jnp.zeros_like(oz[NZ - 1])
    ob = [rcopy(oz.at[(z + k) % NZ], orz.at[k], z_s.at[3, k], z_r.at[3, k], z_dev[k]) for k in range(1, NZ)]
    start(ob)
    contexts(2)
    out_gc = pltpu.make_async_copy(gcv, GC, st.at[1])
    out_gc.start()
    wait(gz)
    gx = [rcopy(gl.at[c, x], gl.at[c, x], x_s.at[1, k], x_r.at[1, k], x_dev[k]) for k in range(1, NX)]
    start(gx)
    wait(ob)
    o3 = oz[z]
    for k in range(1, NZ):
        o3 = o3 + orz[k]
    ol[c, x, z] = o3
    oc = [rcopy(ol.at[c, x, z], ol.at[c, x, z], z_s.at[4, k], z_r.at[4, k], z_dev[k]) for k in range(1, NZ)]
    start(oc)
    wait(gx)
    gc = rcopy(gl.at[c], gl.at[c], c_s.at[1], c_r.at[1], core_dev)
    gc.start()
    wait(oc)
    od = [rcopy(ol.at[c, x], ol.at[c, x], r_s.at[3, e, k], r_r.at[3, e, k], row_dev[e, k]) for e, k in row]
    start(od)
    wait(own_x[:2])
    start(fwd_x[:2])
    gc.wait()
    for p in range(PIECES):
        for i in range(NZ - 1):
            lt[p * PR : (p + 1) * PR, i * 128 : (i + 1) * 128] = gl[p // NX, p % NX, i]
    wait(od)
    for p in range(PIECES):
        for i in range(NZ - 1):
            lt[XR + p * PO : XR + (p + 1) * PO, i * 128 : (i + 1) * 128] = ol[p // NX, p % NX, i, 0:PO, :]
    wait(own_x[2:])
    start(fwd_x[2:])
    q_y = [rcopy(cot.at[0:XC, token_cols(k)], qf.at[SLOT[k]], q_s.at[k], q_r.at[k], y_dev[NY - k]) for k in (1, 3, 2)]
    start(q_y)
    lefts = [lt[b * RANK : (b + 1) * RANK, :] for b in range(NB)]
    inverses = inverse_factors([nt(left, left, PRECISE) for left in lefts])
    for b in range(NB):
        bas[b * RANK : (b + 1) * RANK, :] = nn(inverses[b], lefts[b], PRECISE)

    grads_x(1)
    grads_x(3)
    qf[0] = cot[0:XC, token_cols(0)]
    for i in range(2):
        hi, mid, _ = split3(bas[i * RANK : (i + 2) * RANK, :])
        terms = jnp.concatenate([hi, hi, mid, mid], axis=0).astype(F32)
        bav[i] = terms.T.astype(BF16)
    out_ba = pltpu.make_async_copy(bav, BA, st.at[3])
    out_ba.start()

    rpart[...] = nt(bas[...], acc[...], PRECISE)
    bas3 = jnp.concatenate(split3(bas[...]), axis=0)

    def last_rows(first, size):
        part = nt(bas3, xg[2, first : first + size, :])
        part = jnp.concatenate(split3(part[:NR] + part[NR : 2 * NR] + part[2 * NR :]), axis=0)
        begin = ((y + NY - 2) % NY) * ROWS + first
        part = nt(part, cot[0:XC, pl.ds(pl.multiple_of(begin, 128), size)])
        rpart[:, 0:XC] += part[:NR] + part[NR : 2 * NR] + part[2 * NR :]

    wait(fwd_x[:2])
    last_rows(0, CHR)
    last_rows(3 * CHR, CHR)
    wait(fwd_x[2:])
    last_rows(CHR, 2 * CHR)
    right = jnp.where(in_block((NR, PACK)), rpart[...] * scale, 0.0)
    packed = right[:RANK] + right[RANK : 2 * RANK] + right[2 * RANK :]
    hr = RANK // NC
    for e in range(NC):
        for i in range(NX):
            q1[e, i] = packed[e * hr : (e + 1) * hr, i * 128 : (i + 1) * 128]
    r1 = [rcopy(q1.at[(c + e) % NC, (x + k) % NX], rxr.at[e, k], r_s.at[0, e, k], r_r.at[0, e, k], row_dev[e, k])
          for e, k in row]
    start(r1)
    grads_x(2)
    wait(r1)
    mine = q1[c, x]
    for e, k in row:
        mine = mine + rxr[e, k]
    q2[...] = mine
    r2 = [rcopy(q2, rzr.at[k], z_s.at[2, k], z_r.at[2, k], z_dev[k]) for k in range(1, NZ)]
    start(r2)
    nev[...] = acc[...].T * scale - tn(bas[...], right, PRECISE)
    out_ne = pltpu.make_async_copy(nev, NE, st.at[2])
    out_ne.start()
    wait(r2)
    rzr[0] = q2[...]
    total = rzr[z % NZ]
    for i in range(1, NZ):
        total = total + rzr[(z + NZ - i) % NZ]
    gr[c, x] = total
    r3 = [rcopy(gr.at[c, x], gr.at[c, x], r_s.at[1, e, k], r_r.at[1, e, k], row_dev[e, k]) for e, k in row]
    start(r3)

    w_c.wait()
    wait(q_y[:2])
    near = NY - 1
    gacc[...] = tn(qf[0:near].reshape(near * XC, ROWS), wf[0:near].reshape(near * XC, WL)[:, :D])
    wait(r3)
    out_gr = pltpu.make_async_copy(gr, GR, st.at[4])
    out_gr.start()
    q_y[2].wait()
    giv[...] = (gacc[...] + tn(qf[near], wf[near, :, 0:D])).astype(BF16)
    out_gi = pltpu.make_async_copy(giv, GI, st.at[0])
    out_gi.start()
    wait((out_gc, out_ne, out_ba, out_gi, out_gr))


def finish(GI, GC, NE, BA, GR, gi_out, gc_out, ne_out, cg_out, gi, gc, ne, ba, gr, cg, sem):
    loads = [
        pltpu.make_async_copy(a, b, sem.at[i])
        for i, (a, b) in enumerate(((GR, gr), (BA, ba), (NE, ne), (GI, gi), (GC, gc)))
    ]
    for cp in loads:
        cp.start()
    loads[0].wait()
    hr = RANK // NC
    col = lax.broadcasted_iota(jnp.int32, (RANK, 256), 1)
    rhs = []
    for i, edge in ((0, QC), (1, XC - 256)):
        total = jnp.concatenate(
            [jnp.concatenate([gr[e, 2 * i], gr[e, 2 * i + 1]], axis=1) for e in range(NC)], axis=0
        )
        total = jnp.concatenate([jnp.where(col < edge, total, 0.0), jnp.where(col < edge, 0.0, total)], axis=0)
        hi, mid, _ = split3(total)
        rhs.append(jnp.concatenate([hi, mid, hi, mid], axis=0))
    loads[1].wait()
    stores = []

    def store(src, dst):
        cp = pltpu.make_async_copy(src, dst, sem.at[5 + len(stores)])
        cp.start()
        stores.append(cp)

    half = D // 2
    for r in range(2):
        rows = pl.ds(r * half, half)
        for i in range(2):
            cg[rows, i * 256 : (i + 1) * 256] = nn(ba[i, rows, :], rhs[i])
        store(cg.at[rows], cg_out.at[rows])
    for cp, src, dst in zip(loads[2:], (ne, gi, gc), (ne_out, gi_out, gc_out)):
        cp.wait()
        store(src, dst)
    for cp in stores:
        cp.wait()


def on_device(
    normed_input, grad_query, grad_key, grad_value, context, grad_output,
    w_query, w_key, w_value, w_output, error, factor_init,
):
    any_spec = pl.BlockSpec(memory_space=pl.ANY)
    V = pltpu.VMEM
    hr = RANK // NC
    scratch = [
        V((NY, ROWS, D), BF16), V((NY, ROWS, D), BF16), V((PACK, TOK), BF16),
        V((QC, D), BF16), V((D, PACK), F32), V((RANK, PACK), F32),
        V((NY, XC, WL), BF16), V((NY, XC, ROWS), BF16), V((PACK, D), F32),
        V((NY, XR, ROWS), F32), V((NY, XR, ROWS), F32),
        V((PIECES, NY * PR, D), F32), V((NX, NY * PR, D), F32), V((NX, NY * PR, D), F32),
        V((NX, NY * PR, D), F32), V((NZ, NY * PR, 128), F32), V((NZ, NY * PR, 128), F32),
        V((NY, PR, 128), F32), V((NY, PR, 128), F32), V((NC, NX, NZ, PR, 128), F32),
        V((NR, D), F32), V((NR, D), F32),
        V((NC, NX, 8, D), F32), V((NC, NX, 8, D), F32), V((NZ, 8, 128), F32), V((NZ, 8, 128), F32),
        V((NC, NX, NZ, 8, 128), F32),
        V((NR, PACK), F32), V((NC, NX, hr, 128), F32), V((NC, NX, hr, 128), F32),
        V((hr, 128), F32), V((NZ, hr, 128), F32), V((NC, NX, hr, 128), F32),
        V((ROWS, D), F32), V((ROWS, D), BF16), V((QC, TOK), BF16), V((D, PACK), F32), V((2, D, 256), BF16),
    ]
    S = pltpu.SemaphoreType.DMA
    sems = [
        S((12,)), S((5,)), S((2, 4, CH)), S((2, 4, CH)), S((2, CH)), S((2, CH)), S((NY,)), S((NY,)),
        S((5,)), S((5,)), S((4, NX)), S((4, NX)), S((5, NZ)), S((5, NZ)),
        S((NX,)), S((NX,)), S((2, NY)), S((2, NY)), S((NY,)), S((NY,)),
        S((4, NC, NX)), S((4, NC, NX)),
    ]
    outs = (
        jax.ShapeDtypeStruct((ROWS, D), BF16),
        jax.ShapeDtypeStruct((QC, TOK), BF16),
        jax.ShapeDtypeStruct((D, PACK), F32),
    )
    parts = pl.pallas_call(
        body,
        out_shape=outs[:3] + (
            jax.ShapeDtypeStruct((2, D, 256), BF16),
            jax.ShapeDtypeStruct((NC, NX, hr, 128), F32),
        ),
        in_specs=[any_spec] * 12,
        out_specs=(any_spec,) * 5,
        scratch_shapes=scratch + sems,
        compiler_params=pltpu.CompilerParams(
            collective_id=0, has_side_effects=True, vmem_limit_bytes=60 * 2**20
        ),
        name="backward",
    )(
        normed_input, grad_query.T, grad_key.T, grad_value.T, context.T, grad_output,
        w_query.T, w_key.T, w_value.T, w_output, error, factor_init.T,
    )
    grad_input, grad_context, new_error, compressed = pl.pallas_call(
        finish,
        out_shape=outs + (jax.ShapeDtypeStruct((D, PACK), F32),),
        in_specs=[any_spec] * 5,
        out_specs=(any_spec,) * 4,
        scratch_shapes=[
            V((ROWS, D), BF16), V((QC, TOK), BF16), V((D, PACK), F32),
            V((2, D, 256), BF16), V((NC, NX, hr, 128), F32), V((D, PACK), F32), S((10,)),
        ],
        compiler_params=pltpu.CompilerParams(vmem_limit_bytes=60 * 2**20),
        name="finish",
    )(*parts)
    return grad_input, grad_context.T, new_error, compressed


def solution(mesh):
    return jax.shard_map(
        on_device,
        mesh=mesh,
        in_specs=(
            P(("dp", "tensor"), None),
            P("dp", "tensor"),
            P("dp", "tensor"),
            P("dp", "tensor"),
            P("dp", "tensor"),
            P(("dp", "tensor"), None),
            P(None, "tensor"),
            P(None, "tensor"),
            P(None, "tensor"),
            P("tensor", None),
            P("dp", "tensor"),
            P("tensor", None),
        ),
        out_specs=(
            P(("dp", "tensor"), None),
            P("dp", "tensor"),
            P("dp", "tensor"),
            P(None, "tensor"),
        ),
        check_vma=False,
    )
```

```python
import jax
import jax.numpy as jnp
from jax import lax
from jax.experimental import pallas as pl
from jax.experimental.pallas import tpu as pltpu
from jax.sharding import PartitionSpec as P

MESH = pl.DeviceIdType.MESH
F32, BF16 = jnp.float32, jnp.bfloat16
PRECISE = lax.Precision.HIGHEST
NZ, NX, NC, NY = 8, 4, 2, 4
D = 896
TOK = 2048
ROWS = TOK // NY
CH = 4
CHR = ROWS // CH
QC, KC = 224, 32
PACK = 512
XC = QC + 2 * KC
WL = 1024
WX = WL // NX
SLOT = (0, 1, 3, 2)
RANK = 32
NB = 3
NR = NB * RANK
PIECES = NC * NX
XR = 2 * RANK
PR = XR // PIECES
PO = RANK // PIECES
WR = XC // NC


def nt(a, b, precision=None):
    return lax.dot_general(
        a, b, (((1,), (1,)), ((), ())), precision=precision, preferred_element_type=F32
    )


def tn(a, b, precision=None):
    return lax.dot_general(
        a, b, (((0,), (0,)), ((), ())), precision=precision, preferred_element_type=F32
    )


def nn(a, b, precision=None):
    return jnp.dot(a, b, precision=precision, preferred_element_type=F32)


def split3(a):
    hi = a.astype(BF16)
    rest = a - hi.astype(F32)
    mid = rest.astype(BF16)
    low = (rest - mid.astype(F32)).astype(BF16)
    return hi, mid, low


def in_block(shape):
    row = lax.broadcasted_iota(jnp.int32, shape, 0)
    col = lax.broadcasted_iota(jnp.int32, shape, 1)
    block = (col >= QC).astype(jnp.int32) + (col >= XC).astype(jnp.int32)
    return (row // RANK) == block


def rcopy(src, dst, send, recv, dev):
    return pltpu.make_async_remote_copy(
        src_ref=src, dst_ref=dst, send_sem=send, recv_sem=recv, device_id=dev, device_id_type=MESH
    )


def inverse_factors(grams):
    row = lax.broadcasted_iota(jnp.int32, (RANK, RANK), 0)
    col = lax.broadcasted_iota(jnp.int32, (RANK, RANK), 1)
    eye = (row == col).astype(F32)
    works = [jnp.concatenate([eye, gram], axis=1) for gram in grams]
    sub = lax.broadcasted_iota(jnp.int32, (RANK, 2 * RANK), 0)
    for k in range(RANK):
        for b, work in enumerate(works):
            pivot = work[k : k + 1, RANK + k : RANK + k + 1]
            inv = 1.0 / jnp.sqrt(pivot)
            row_k = work[k : k + 1, :] * inv
            col_k = work[:, RANK + k : RANK + k + 1] * inv
            works[b] = jnp.where(sub > k, work - col_k * row_k, jnp.where(sub == k, row_k, work))
    return [work[:, :RANK] for work in works]


def body(
    X, DQ, DK, DV, CX, DO, WQ, WK, WV, WO, ER, FI,
    GI, GC, NE, BA, GR,
    xg, og, cot, wo, er, fi, wf, qf, acc,
    pts, ptr, lts, rcore, s1, rx, sz, rz, sy, ry, gl, lt, bas,
    o1, orx, oz, orz, ol,
    rpart, q1, rxr, q2, rzr, gr,
    gacc, giv, gcv, nev, bav,
    ld, st, ag_s, ag_r, fw_s, fw_r, p_s, p_r, c_s, c_r, x_s, x_r, z_s, z_r, w_s, w_r, y_s, y_r, q_s, q_r, r_s, r_r,
):
    d = lax.axis_index("dp")
    y = lax.axis_index("tensor")
    z, x, c = d // (NX * NC), (d // NC) % NX, d % NC

    def dev(z_, x_, c_, y_):
        return ((z_ * NX + x_) * NC + c_, y_)

    core_dev = dev(z, x, 1 - c, y)
    x_dev = [dev(z, (x + k) % NX, c, y) for k in range(NX)]
    z_dev = [dev((z + k) % NZ, x, c, y) for k in range(NZ)]
    y_dev = [dev(z, x, c, (y + k) % NY) for k in range(NY)]
    row = [(e, k) for k in (2, 1, 3, 0) for e in range(NC) if e + k > 0]
    row_dev = {(e, k): dev(z, (x + k) % NX, (c + e) % NC, y) for e, k in row}

    def start(copies):
        for cp in copies:
            cp.start()

    def wait(copies):
        for cp in copies:
            cp.wait()

    barrier = pltpu.get_barrier_semaphore()
    peers = [z_dev[k] for k in (4, 3, 5, 2, 6, 1, 7)] + list(row_dev.values()) + y_dev[1:]
    for p in peers:
        pl.semaphore_signal(barrier, inc=1, device_id=p, device_id_type=MESH)

    pairs = [
        (WQ, wf.at[0, 0:QC, 0:D]), (WK, wf.at[0, QC : QC + KC, 0:D]), (WV, wf.at[0, QC + KC : XC, 0:D]),
        (DQ, cot.at[0:QC]), (DK, cot.at[QC : QC + KC]), (DV, cot.at[QC + KC : XC]), (CX, cot.at[XC:PACK]),
        (FI, fi), (ER, er), (X, xg.at[0]), (DO, og.at[0]), (WO, wo),
    ]
    loads = [pltpu.make_async_copy(a, b, ld.at[i]) for i, (a, b) in enumerate(pairs)]
    start(loads)
    wf[0, :, D:] = jnp.zeros((XC, WL - D), BF16)
    pl.semaphore_wait(barrier, len(peers))

    def own_sends(i, src, dst):
        out = []
        for n in range(CH):
            for way, h in ((1, n), (3, CH - 1 - n)):
                rows = pl.ds(h * CHR, CHR)
                out.append(rcopy(src.at[rows], dst.at[way, rows],
                                 ag_s.at[i, way, h], ag_r.at[i, way, h], y_dev[way]))
        return out

    def forwards(i, buf):
        out = []
        for n in range(CH // 2):
            for way, h in ((1, n), (3, CH - 1 - n)):
                rows = pl.ds(h * CHR, CHR)
                out.append(rcopy(buf.at[way, rows], buf.at[2, rows], fw_s.at[i, h], fw_r.at[i, h], y_dev[way]))
        return out

    own_o, own_x = own_sends(0, DO, og), own_sends(1, X, xg)
    fwd_o, fwd_x = forwards(0, og), forwards(1, xg)
    start(own_o[:2])

    wrows, wcols = pl.ds(pl.multiple_of(c * WR, 16), WR), pl.ds(pl.multiple_of(x * WX, 128), WX)
    odd = z % 2
    wtile = pl.ds(pl.multiple_of(x * WX + odd * (WX // 2), 128), WX // 2)
    w_y = [rcopy(wf.at[0, wrows, wtile], wf.at[SLOT[k], wrows, wtile], y_s.at[1, k], y_r.at[1, k], y_dev[NY - k])
           for k in range(1, NY)]
    wait(loads[:3])
    start(w_y)

    wait(loads[3:8])
    fm = jnp.where(in_block((NR, PACK)), jnp.concatenate([fi[...]] * NB, axis=0), 0.0)
    fm3 = jnp.concatenate(split3(fm[:XR, :XC]), axis=0)

    def token_cols(k):
        return pl.ds(pl.multiple_of(((y + NY - k) % NY) * ROWS, ROWS), ROWS)

    for k in (1, 3, 2, 0):
        prod = nn(fm3, cot[0:XC, token_cols(k)])
        dst = ptr if k == 0 else pts
        dst[k] = prod[:XR] + prod[XR : 2 * XR] + prod[2 * XR :]
    p_y = [rcopy(pts.at[k], ptr.at[k], p_s.at[k], p_r.at[k], y_dev[NY - k]) for k in (1, 3, 2)]
    start(p_y)

    start(own_o[2:])

    wait(w_y)
    w_z = rcopy(wf.at[pl.ds(1, NY - 1), wrows, wtile], wf.at[pl.ds(1, NY - 1), wrows, wtile],
                w_s.at[0], w_r.at[0], dev(z + 1 - 2 * odd, x, c, y))
    w_z.start()
    w_x = [rcopy(wf.at[pl.ds(1, NY - 1), wrows, wcols], wf.at[pl.ds(1, NY - 1), wrows, wcols],
                 w_s.at[k], w_r.at[k], x_dev[k]) for k in range(1, NX)]

    def grads_x(slot):
        acc[0:XC, :] += nn(cot[0:XC, token_cols(slot)], xg[slot])

    def grads_o(slot):
        acc[XC:PACK, :] += nn(cot[XC:PACK, token_cols(slot)], og[slot])

    def contexts(slot):
        gcv[:, token_cols(slot)] = nt(wo[...], og[slot]).astype(BF16)

    scale = float(TOK) ** (-0.5)
    wait(loads[8:])
    own_e = nt(fm[:XR], er[...], PRECISE)
    acc[...] = er[...].T * (float(TOK) ** 0.5)
    w_z.wait()
    start(w_x)
    grads_x(0)
    grads_o(0)
    contexts(0)

    def left_from(k):
        left = nn(jnp.concatenate(split3(ptr[k]), axis=0), xg[0])
        left = (left[:XR] + left[XR : 2 * XR] + left[2 * XR :]) * scale
        if k == 0:
            left = left + own_e
        for p in range(PIECES):
            lts[p, k * PR : (k + 1) * PR, :] = left[p * PR : (p + 1) * PR, :]

    left_from(0)
    for cp, k in zip(p_y, (1, 3, 2)):
        cp.wait()
        left_from(k)

    wait(own_o[:2])
    start(fwd_o[:2])

    lc = rcopy(lts.at[pl.ds(NX * (1 - c), NX)], rcore, c_s.at[0], c_r.at[0], core_dev)
    lc.start()
    wait(w_x)
    w_c = rcopy(wf.at[pl.ds(1, NY - 1), wrows], wf.at[pl.ds(1, NY - 1), wrows], c_s.at[4], c_r.at[4], core_dev)
    lc.wait()
    w_c.start()
    s1[...] = lts[pl.ds(NX * c, NX)] + rcore[...]
    lx = [rcopy(s1.at[(x + k) % NX], rx.at[k], x_s.at[0, k], x_r.at[0, k], x_dev[k]) for k in range(1, NX)]
    start(lx)
    wait(own_o[2:])
    start(fwd_o[2:])
    start(own_x[:2])
    grads_o(1)
    wait(lx)
    s2 = s1[x] + rx[1] + rx[2] + rx[3]
    for i in range(NZ - 1):
        sz[i] = s2[:, i * 128 : (i + 1) * 128]
    sz[NZ - 1] = jnp.zeros_like(sz[NZ - 1])
    lz = [rcopy(sz.at[(z + k) % NZ], rz.at[k], z_s.at[0, k], z_r.at[0, k], z_dev[k]) for k in range(1, NZ)]
    start(lz)
    wait(lz)
    s3 = sz[z]
    for k in range(1, NZ):
        s3 = s3 + rz[k]
    for k in range(NY):
        sy[k] = s3[k * PR : (k + 1) * PR, :]
    ly = [rcopy(sy.at[k], ry.at[k], y_s.at[0, k], y_r.at[0, k], y_dev[k]) for k in range(1, NY)]
    start(ly)
    start(own_x[2:])
    grads_o(3)
    contexts(1)

    wait(fwd_o)
    grads_o(2)
    left_o = nn(fm[XR:], acc[...], PRECISE) * scale
    for p in range(PIECES):
        o1[p // NX, p % NX, 0:PO, :] = left_o[p * PO : (p + 1) * PO, :]
        o1[p // NX, p % NX, PO:, :] = jnp.zeros((8 - PO, D), F32)
    oa = [rcopy(o1.at[(c + e) % NC, (x + k) % NX], orx.at[e, k], r_s.at[2, e, k], r_r.at[2, e, k], row_dev[e, k])
          for e, k in row]
    start(oa)
    contexts(3)
    wait(ly)
    gl[c, x, z] = sy[0] + ry[1] + ry[2] + ry[3]
    gz = [rcopy(gl.at[c, x, z], gl.at[c, x, z], z_s.at[1, k], z_r.at[1, k], z_dev[k]) for k in range(1, NZ)]
    start(gz)
    wait(oa)
    o2 = o1[c, x]
    for e, k in row:
        o2 = o2 + orx[e, k]
    for i in range(NZ - 1):
        oz[i] = o2[:, i * 128 : (i + 1) * 128]
    oz[NZ - 1] = jnp.zeros_like(oz[NZ - 1])
    ob = [rcopy(oz.at[(z + k) % NZ], orz.at[k], z_s.at[3, k], z_r.at[3, k], z_dev[k]) for k in range(1, NZ)]
    start(ob)
    wait(own_x[:2])
    start(fwd_x[:2])
    contexts(2)
    out_gc = pltpu.make_async_copy(gcv, GC, st.at[1])
    out_gc.start()
    wait(gz)
    gx = [rcopy(gl.at[c, x], gl.at[c, x], x_s.at[1, k], x_r.at[1, k], x_dev[k]) for k in range(1, NX)]
    start(gx)
    wait(ob)
    o3 = oz[z]
    for k in range(1, NZ):
        o3 = o3 + orz[k]
    ol[c, x, z] = o3
    oc = [rcopy(ol.at[c, x, z], ol.at[c, x, z], z_s.at[4, k], z_r.at[4, k], z_dev[k]) for k in range(1, NZ)]
    start(oc)
    wait(gx)
    gc = rcopy(gl.at[c], gl.at[c], c_s.at[1], c_r.at[1], core_dev)
    gc.start()
    wait(oc)
    od = [rcopy(ol.at[c, x], ol.at[c, x], r_s.at[3, e, k], r_r.at[3, e, k], row_dev[e, k]) for e, k in row]
    start(od)
    wait(own_x[2:])
    start(fwd_x[2:])
    q_y = [rcopy(cot.at[0:XC, token_cols(k)], qf.at[SLOT[k]], q_s.at[k], q_r.at[k], y_dev[NY - k]) for k in (1, 3, 2)]
    start(q_y)
    gc.wait()
    for p in range(PIECES):
        for i in range(NZ - 1):
            lt[p * PR : (p + 1) * PR, i * 128 : (i + 1) * 128] = gl[p // NX, p % NX, i]
    wait(od)
    for p in range(PIECES):
        for i in range(NZ - 1):
            lt[XR + p * PO : XR + (p + 1) * PO, i * 128 : (i + 1) * 128] = ol[p // NX, p % NX, i, 0:PO, :]
    lefts = [lt[b * RANK : (b + 1) * RANK, :] for b in range(NB)]
    inverses = inverse_factors([nt(left, left, PRECISE) for left in lefts])
    for b in range(NB):
        bas[b * RANK : (b + 1) * RANK, :] = nn(inverses[b], lefts[b], PRECISE)

    grads_x(1)
    grads_x(3)
    qf[0] = cot[0:XC, token_cols(0)]
    for i in range(2):
        hi, mid, _ = split3(bas[i * RANK : (i + 2) * RANK, :])
        terms = jnp.concatenate([hi, hi, mid, mid], axis=0).astype(F32)
        bav[i] = terms.T.astype(BF16)
    out_ba = pltpu.make_async_copy(bav, BA, st.at[3])
    out_ba.start()

    rpart[...] = nt(bas[...], acc[...], PRECISE)
    bas3 = jnp.concatenate(split3(bas[...]), axis=0)

    def last_rows(first, size):
        part = nt(bas3, xg[2, first : first + size, :])
        part = jnp.concatenate(split3(part[:NR] + part[NR : 2 * NR] + part[2 * NR :]), axis=0)
        begin = ((y + NY - 2) % NY) * ROWS + first
        part = nt(part, cot[0:XC, pl.ds(pl.multiple_of(begin, 128), size)])
        rpart[:, 0:XC] += part[:NR] + part[NR : 2 * NR] + part[2 * NR :]

    wait(fwd_x[:2])
    last_rows(0, CHR)
    last_rows(3 * CHR, CHR)
    wait(fwd_x[2:])
    last_rows(CHR, 2 * CHR)
    right = jnp.where(in_block((NR, PACK)), rpart[...] * scale, 0.0)
    packed = right[:RANK] + right[RANK : 2 * RANK] + right[2 * RANK :]
    hr = RANK // NC
    for e in range(NC):
        for i in range(NX):
            q1[e, i] = packed[e * hr : (e + 1) * hr, i * 128 : (i + 1) * 128]
    r1 = [rcopy(q1.at[(c + e) % NC, (x + k) % NX], rxr.at[e, k], r_s.at[0, e, k], r_r.at[0, e, k], row_dev[e, k])
          for e, k in row]
    start(r1)
    grads_x(2)
    wait(r1)
    mine = q1[c, x]
    for e, k in row:
        mine = mine + rxr[e, k]
    q2[...] = mine
    r2 = [rcopy(q2, rzr.at[k], z_s.at[2, k], z_r.at[2, k], z_dev[k]) for k in (4, 3, 5, 2, 6, 1, 7)]
    start(r2)
    nev[...] = acc[...].T * scale - tn(bas[...], right, PRECISE)
    out_ne = pltpu.make_async_copy(nev, NE, st.at[2])
    out_ne.start()
    wait(r2)
    rzr[0] = q2[...]
    total = rzr[z % NZ]
    for i in range(1, NZ):
        total = total + rzr[(z + NZ - i) % NZ]
    gr[c, x] = total
    r3 = [rcopy(gr.at[c, x], GR.at[c, x], r_s.at[1, e, k], r_r.at[1, e, k], row_dev[e, k]) for e, k in row]
    start(r3)
    out_gr = pltpu.make_async_copy(gr.at[c, x], GR.at[c, x], st.at[4])
    out_gr.start()

    w_c.wait()
    wait(q_y[:2])
    near = NY - 1
    gacc[...] = tn(qf[0:near].reshape(near * XC, ROWS), wf[0:near].reshape(near * XC, WL)[:, :D])
    q_y[2].wait()
    giv[...] = (gacc[...] + tn(qf[near], wf[near, :, 0:D])).astype(BF16)
    out_gi = pltpu.make_async_copy(giv, GI, st.at[0])
    out_gi.start()
    wait(r3)
    wait((out_gc, out_ne, out_ba, out_gi, out_gr))


def finish(GI, GC, NE, BA, GR, gi_out, gc_out, ne_out, cg_out, gi, gc, ne, ba, gr, cg, sem):
    loads = [
        pltpu.make_async_copy(a, b, sem.at[i])
        for i, (a, b) in enumerate(((GR, gr), (BA, ba), (NE, ne), (GI, gi), (GC, gc)))
    ]
    for cp in loads:
        cp.start()
    loads[0].wait()
    hr = RANK // NC
    col = lax.broadcasted_iota(jnp.int32, (RANK, 256), 1)
    rhs = []
    for i, edge in ((0, QC), (1, XC - 256)):
        total = jnp.concatenate(
            [jnp.concatenate([gr[e, 2 * i], gr[e, 2 * i + 1]], axis=1) for e in range(NC)], axis=0
        )
        total = jnp.concatenate([jnp.where(col < edge, total, 0.0), jnp.where(col < edge, 0.0, total)], axis=0)
        hi, mid, _ = split3(total)
        rhs.append(jnp.concatenate([hi, mid, hi, mid], axis=0))
    loads[1].wait()
    stores = []

    def store(src, dst):
        cp = pltpu.make_async_copy(src, dst, sem.at[5 + len(stores)])
        cp.start()
        stores.append(cp)

    half = D // 2
    for r in range(2):
        rows = pl.ds(r * half, half)
        for i in range(2):
            cg[rows, i * 256 : (i + 1) * 256] = nn(ba[i, rows, :], rhs[i])
        store(cg.at[rows], cg_out.at[rows])
    for cp, src, dst in zip(loads[2:], (ne, gi, gc), (ne_out, gi_out, gc_out)):
        cp.wait()
        store(src, dst)
    for cp in stores:
        cp.wait()


def on_device(
    normed_input, grad_query, grad_key, grad_value, context, grad_output,
    w_query, w_key, w_value, w_output, error, factor_init,
):
    any_spec = pl.BlockSpec(memory_space=pl.ANY)
    V = pltpu.VMEM
    hr = RANK // NC
    scratch = [
        V((NY, ROWS, D), BF16), V((NY, ROWS, D), BF16), V((PACK, TOK), BF16),
        V((QC, D), BF16), V((D, PACK), F32), V((RANK, PACK), F32),
        V((NY, XC, WL), BF16), V((NY, XC, ROWS), BF16), V((PACK, D), F32),
        V((NY, XR, ROWS), F32), V((NY, XR, ROWS), F32),
        V((PIECES, NY * PR, D), F32), V((NX, NY * PR, D), F32), V((NX, NY * PR, D), F32),
        V((NX, NY * PR, D), F32), V((NZ, NY * PR, 128), F32), V((NZ, NY * PR, 128), F32),
        V((NY, PR, 128), F32), V((NY, PR, 128), F32), V((NC, NX, NZ, PR, 128), F32),
        V((NR, D), F32), V((NR, D), F32),
        V((NC, NX, 8, D), F32), V((NC, NX, 8, D), F32), V((NZ, 8, 128), F32), V((NZ, 8, 128), F32),
        V((NC, NX, NZ, 8, 128), F32),
        V((NR, PACK), F32), V((NC, NX, hr, 128), F32), V((NC, NX, hr, 128), F32),
        V((hr, 128), F32), V((NZ, hr, 128), F32), V((NC, NX, hr, 128), F32),
        V((ROWS, D), F32), V((ROWS, D), BF16), V((QC, TOK), BF16), V((D, PACK), F32), V((2, D, 256), BF16),
    ]
    S = pltpu.SemaphoreType.DMA
    sems = [
        S((12,)), S((5,)), S((2, 4, CH)), S((2, 4, CH)), S((2, CH)), S((2, CH)), S((NY,)), S((NY,)),
        S((5,)), S((5,)), S((4, NX)), S((4, NX)), S((5, NZ)), S((5, NZ)),
        S((NX,)), S((NX,)), S((2, NY)), S((2, NY)), S((NY,)), S((NY,)),
        S((4, NC, NX)), S((4, NC, NX)),
    ]
    outs = (
        jax.ShapeDtypeStruct((ROWS, D), BF16),
        jax.ShapeDtypeStruct((QC, TOK), BF16),
        jax.ShapeDtypeStruct((D, PACK), F32),
    )
    parts = pl.pallas_call(
        body,
        out_shape=outs[:3] + (
            jax.ShapeDtypeStruct((2, D, 256), BF16),
            jax.ShapeDtypeStruct((NC, NX, hr, 128), F32),
        ),
        in_specs=[any_spec] * 12,
        out_specs=(any_spec,) * 5,
        scratch_shapes=scratch + sems,
        compiler_params=pltpu.CompilerParams(
            collective_id=0, has_side_effects=True, vmem_limit_bytes=60 * 2**20
        ),
        name="backward",
    )(
        normed_input, grad_query.T, grad_key.T, grad_value.T, context.T, grad_output,
        w_query.T, w_key.T, w_value.T, w_output, error, factor_init.T,
    )
    grad_input, grad_context, new_error, compressed = pl.pallas_call(
        finish,
        out_shape=outs + (jax.ShapeDtypeStruct((D, PACK), F32),),
        in_specs=[any_spec] * 5,
        out_specs=(any_spec,) * 4,
        scratch_shapes=[
            V((ROWS, D), BF16), V((QC, TOK), BF16), V((D, PACK), F32),
            V((2, D, 256), BF16), V((NC, NX, hr, 128), F32), V((D, PACK), F32), S((10,)),
        ],
        compiler_params=pltpu.CompilerParams(vmem_limit_bytes=60 * 2**20),
        name="finish",
    )(*parts)
    return grad_input, grad_context.T, new_error, compressed


def solution(mesh):
    return jax.shard_map(
        on_device,
        mesh=mesh,
        in_specs=(
            P(("dp", "tensor"), None),
            P("dp", "tensor"),
            P("dp", "tensor"),
            P("dp", "tensor"),
            P("dp", "tensor"),
            P(("dp", "tensor"), None),
            P(None, "tensor"),
            P(None, "tensor"),
            P(None, "tensor"),
            P("tensor", None),
            P("dp", "tensor"),
            P("tensor", None),
        ),
        out_specs=(
            P(("dp", "tensor"), None),
            P("dp", "tensor"),
            P("dp", "tensor"),
            P(None, "tensor"),
        ),
        check_vma=False,
    )
```

```python
import jax
import jax.numpy as jnp
from jax import lax
from jax.experimental import pallas as pl
from jax.experimental.pallas import tpu as pltpu
from jax.sharding import PartitionSpec as P

MESH = pl.DeviceIdType.MESH
F32, BF16 = jnp.float32, jnp.bfloat16
PRECISE = lax.Precision.HIGHEST
NZ, NX, NC, NY = 8, 4, 2, 4
D = 896
TOK = 2048
ROWS = TOK // NY
CH = 4
CHR = ROWS // CH
QC, KC = 224, 32
PACK = 512
XC = QC + 2 * KC
WL = 1024
WX = WL // NX
SLOT = (0, 1, 3, 2)
RANK = 32
NB = 3
NR = NB * RANK
PIECES = NC * NX
XR = 2 * RANK
PR = XR // PIECES
PO = RANK // PIECES
WR = XC // NC


def nt(a, b, precision=None):
    return lax.dot_general(
        a, b, (((1,), (1,)), ((), ())), precision=precision, preferred_element_type=F32
    )


def tn(a, b, precision=None):
    return lax.dot_general(
        a, b, (((0,), (0,)), ((), ())), precision=precision, preferred_element_type=F32
    )


def nn(a, b, precision=None):
    return jnp.dot(a, b, precision=precision, preferred_element_type=F32)


def split3(a):
    hi = a.astype(BF16)
    rest = a - hi.astype(F32)
    mid = rest.astype(BF16)
    low = (rest - mid.astype(F32)).astype(BF16)
    return hi, mid, low


def in_block(shape):
    row = lax.broadcasted_iota(jnp.int32, shape, 0)
    col = lax.broadcasted_iota(jnp.int32, shape, 1)
    block = (col >= QC).astype(jnp.int32) + (col >= XC).astype(jnp.int32)
    return (row // RANK) == block


def rcopy(src, dst, send, recv, dev):
    return pltpu.make_async_remote_copy(
        src_ref=src, dst_ref=dst, send_sem=send, recv_sem=recv, device_id=dev, device_id_type=MESH
    )


def inverse_factors(grams):
    row = lax.broadcasted_iota(jnp.int32, (RANK, RANK), 0)
    col = lax.broadcasted_iota(jnp.int32, (RANK, RANK), 1)
    eye = (row == col).astype(F32)
    works = [jnp.concatenate([eye, gram], axis=1) for gram in grams]
    sub = lax.broadcasted_iota(jnp.int32, (RANK, 2 * RANK), 0)
    for k in range(RANK):
        for b, work in enumerate(works):
            pivot = work[k : k + 1, RANK + k : RANK + k + 1]
            inv = 1.0 / jnp.sqrt(pivot)
            row_k = work[k : k + 1, :] * inv
            col_k = work[:, RANK + k : RANK + k + 1] * inv
            works[b] = jnp.where(sub > k, work - col_k * row_k, jnp.where(sub == k, row_k, work))
    return [work[:, :RANK] for work in works]


def body(
    X, DQ, DK, DV, CX, DO, WQ, WK, WV, WO, ER, FI,
    GI, GC, NE, BA, GR,
    xg, og, cot, wo, er, fi, wf, qf, acc,
    pts, ptr, lts, rcore, s1, rx, sz, rz, sy, ry, gl, lt, bas,
    o1, orx, oz, orz, ol,
    rpart, q1, rxr, q2, rzr, gr,
    gacc, giv, gcv, nev, bav,
    ld, st, ag_s, ag_r, fw_s, fw_r, p_s, p_r, c_s, c_r, x_s, x_r, z_s, z_r, w_s, w_r, y_s, y_r, q_s, q_r, r_s, r_r,
):
    d = lax.axis_index("dp")
    y = lax.axis_index("tensor")
    z, x, c = d // (NX * NC), (d // NC) % NX, d % NC

    def dev(z_, x_, c_, y_):
        return ((z_ * NX + x_) * NC + c_, y_)

    core_dev = dev(z, x, 1 - c, y)
    x_dev = [dev(z, (x + k) % NX, c, y) for k in range(NX)]
    z_dev = [dev((z + k) % NZ, x, c, y) for k in range(NZ)]
    y_dev = [dev(z, x, c, (y + k) % NY) for k in range(NY)]
    row = [(e, k) for k in (2, 1, 3, 0) for e in range(NC) if e + k > 0]
    row_dev = {(e, k): dev(z, (x + k) % NX, (c + e) % NC, y) for e, k in row}

    def start(copies):
        for cp in copies:
            cp.start()

    def wait(copies):
        for cp in copies:
            cp.wait()

    barrier = pltpu.get_barrier_semaphore()
    peers = [z_dev[k] for k in (4, 3, 5, 2, 6, 1, 7)] + list(row_dev.values()) + y_dev[1:]
    for p in peers:
        pl.semaphore_signal(barrier, inc=1, device_id=p, device_id_type=MESH)

    pairs = [
        (WQ, wf.at[0, 0:QC, 0:D]), (WK, wf.at[0, QC : QC + KC, 0:D]), (WV, wf.at[0, QC + KC : XC, 0:D]),
        (DQ, cot.at[0:QC]), (DK, cot.at[QC : QC + KC]), (DV, cot.at[QC + KC : XC]), (CX, cot.at[XC:PACK]),
        (FI, fi), (ER, er), (X, xg.at[0]), (DO, og.at[0]), (WO, wo),
    ]
    loads = [pltpu.make_async_copy(a, b, ld.at[i]) for i, (a, b) in enumerate(pairs)]
    start(loads)
    wf[0, :, D:] = jnp.zeros((XC, WL - D), BF16)
    pl.semaphore_wait(barrier, len(peers))

    def own_sends(i, src, dst):
        out = []
        for n in range(CH):
            for way, h in ((1, n), (3, CH - 1 - n)):
                rows = pl.ds(h * CHR, CHR)
                out.append(rcopy(src.at[rows], dst.at[way, rows],
                                 ag_s.at[i, way, h], ag_r.at[i, way, h], y_dev[way]))
        return out

    def forwards(i, buf):
        out = []
        for n in range(CH // 2):
            for way, h in ((1, n), (3, CH - 1 - n)):
                rows = pl.ds(h * CHR, CHR)
                out.append(rcopy(buf.at[way, rows], buf.at[2, rows], fw_s.at[i, h], fw_r.at[i, h], y_dev[way]))
        return out

    own_o, own_x = own_sends(0, DO, og), own_sends(1, X, xg)
    fwd_o, fwd_x = forwards(0, og), forwards(1, xg)
    start(own_o[:2])

    wrows, wcols = pl.ds(pl.multiple_of(c * WR, 16), WR), pl.ds(pl.multiple_of(x * WX, 128), WX)
    odd = z % 2
    wtile = pl.ds(pl.multiple_of(x * WX + odd * (WX // 2), 128), WX // 2)
    w_y = [rcopy(wf.at[0, wrows, wtile], wf.at[SLOT[k], wrows, wtile], y_s.at[1, k], y_r.at[1, k], y_dev[NY - k])
           for k in range(1, NY)]
    wait(loads[:3])
    start(w_y)

    wait(loads[3:8])
    fm = jnp.where(in_block((NR, PACK)), jnp.concatenate([fi[...]] * NB, axis=0), 0.0)
    fm3 = jnp.concatenate(split3(fm[:XR, :XC]), axis=0)

    def token_cols(k):
        return pl.ds(pl.multiple_of(((y + NY - k) % NY) * ROWS, ROWS), ROWS)

    for k in (1, 3, 2, 0):
        prod = nn(fm3, cot[0:XC, token_cols(k)])
        dst = ptr if k == 0 else pts
        dst[k] = prod[:XR] + prod[XR : 2 * XR] + prod[2 * XR :]
    p_y = [rcopy(pts.at[k], ptr.at[k], p_s.at[k], p_r.at[k], y_dev[NY - k]) for k in (1, 3, 2)]
    start(p_y)

    start(own_o[2:])

    wait(w_y)
    w_z = rcopy(wf.at[pl.ds(1, NY - 1), wrows, wtile], wf.at[pl.ds(1, NY - 1), wrows, wtile],
                w_s.at[0], w_r.at[0], dev(z + 1 - 2 * odd, x, c, y))
    w_z.start()
    w_x = [rcopy(wf.at[pl.ds(1, NY - 1), wrows, wcols], wf.at[pl.ds(1, NY - 1), wrows, wcols],
                 w_s.at[k], w_r.at[k], x_dev[k]) for k in range(1, NX)]

    def grads_x(slot):
        acc[0:XC, :] += nn(cot[0:XC, token_cols(slot)], xg[slot])

    def grads_o(slot):
        acc[XC:PACK, :] += nn(cot[XC:PACK, token_cols(slot)], og[slot])

    def contexts(slot):
        gcv[:, token_cols(slot)] = nt(wo[...], og[slot]).astype(BF16)

    scale = float(TOK) ** (-0.5)
    wait(loads[8:])
    own_e = nt(fm[:XR], er[...], PRECISE)
    acc[...] = er[...].T * (float(TOK) ** 0.5)
    w_z.wait()
    start(w_x)
    grads_x(0)
    grads_o(0)
    contexts(0)

    def left_from(k):
        left = nn(jnp.concatenate(split3(ptr[k]), axis=0), xg[0])
        left = (left[:XR] + left[XR : 2 * XR] + left[2 * XR :]) * scale
        if k == 0:
            left = left + own_e
        for p in range(PIECES):
            lts[p, k * PR : (k + 1) * PR, :] = left[p * PR : (p + 1) * PR, :]

    left_from(0)
    for cp, k in zip(p_y, (1, 3, 2)):
        cp.wait()
        left_from(k)

    wait(own_o[:2])
    start(fwd_o[:2])

    lc = rcopy(lts.at[pl.ds(NX * (1 - c), NX)], rcore, c_s.at[0], c_r.at[0], core_dev)
    lc.start()
    wait(w_x)
    w_c = rcopy(wf.at[pl.ds(1, NY - 1), wrows], wf.at[pl.ds(1, NY - 1), wrows], c_s.at[4], c_r.at[4], core_dev)
    lc.wait()
    w_c.start()
    s1[...] = lts[pl.ds(NX * c, NX)] + rcore[...]
    lx = [rcopy(s1.at[(x + k) % NX], rx.at[k], x_s.at[0, k], x_r.at[0, k], x_dev[k]) for k in range(1, NX)]
    start(lx)
    wait(own_o[2:])
    start(fwd_o[2:])
    start(own_x[:2])
    grads_o(1)
    wait(lx)
    s2 = s1[x] + rx[1] + rx[2] + rx[3]
    for i in range(NZ - 1):
        sz[i] = s2[:, i * 128 : (i + 1) * 128]
    sz[NZ - 1] = jnp.zeros_like(sz[NZ - 1])
    lz = [rcopy(sz.at[(z + k) % NZ], rz.at[k], z_s.at[0, k], z_r.at[0, k], z_dev[k]) for k in range(1, NZ)]
    start(lz)
    wait(lz)
    s3 = sz[z]
    for k in range(1, NZ):
        s3 = s3 + rz[k]
    for k in range(NY):
        sy[k] = s3[k * PR : (k + 1) * PR, :]
    ly = [rcopy(sy.at[k], ry.at[k], y_s.at[0, k], y_r.at[0, k], y_dev[k]) for k in range(1, NY)]
    start(ly)
    start(own_x[2:])
    grads_o(3)
    contexts(1)

    wait(fwd_o)
    grads_o(2)
    left_o = nn(fm[XR:], acc[...], PRECISE) * scale
    for p in range(PIECES):
        o1[p // NX, p % NX, 0:PO, :] = left_o[p * PO : (p + 1) * PO, :]
        o1[p // NX, p % NX, PO:, :] = jnp.zeros((8 - PO, D), F32)
    oa = [rcopy(o1.at[(c + e) % NC, (x + k) % NX], orx.at[e, k], r_s.at[2, e, k], r_r.at[2, e, k], row_dev[e, k])
          for e, k in row]
    start(oa)
    contexts(3)
    wait(ly)
    gl[c, x, z] = sy[0] + ry[1] + ry[2] + ry[3]
    gz = [rcopy(gl.at[c, x, z], gl.at[c, x, z], z_s.at[1, k], z_r.at[1, k], z_dev[k]) for k in range(1, NZ)]
    start(gz)
    wait(oa)
    o2 = o1[c, x]
    for e, k in row:
        o2 = o2 + orx[e, k]
    for i in range(NZ - 1):
        oz[i] = o2[:, i * 128 : (i + 1) * 128]
    oz[NZ - 1] = jnp.zeros_like(oz[NZ - 1])
    ob = [rcopy(oz.at[(z + k) % NZ], orz.at[k], z_s.at[3, k], z_r.at[3, k], z_dev[k]) for k in range(1, NZ)]
    start(ob)
    wait(own_x[:2])
    start(fwd_x[:2])
    contexts(2)
    out_gc = pltpu.make_async_copy(gcv, GC, st.at[1])
    out_gc.start()
    wait(gz)
    gx = [rcopy(gl.at[c, x], gl.at[c, x], x_s.at[1, k], x_r.at[1, k], x_dev[k]) for k in range(1, NX)]
    start(gx)
    wait(ob)
    o3 = oz[z]
    for k in range(1, NZ):
        o3 = o3 + orz[k]
    ol[c, x, z] = o3
    oc = [rcopy(ol.at[c, x, z], ol.at[c, x, z], z_s.at[4, k], z_r.at[4, k], z_dev[k]) for k in range(1, NZ)]
    start(oc)
    wait(gx)
    gc = rcopy(gl.at[c], gl.at[c], c_s.at[1], c_r.at[1], core_dev)
    gc.start()
    wait(oc)
    od = [rcopy(ol.at[c, x], ol.at[c, x], r_s.at[3, e, k], r_r.at[3, e, k], row_dev[e, k]) for e, k in row]
    start(od)
    wait(own_x[2:])
    start(fwd_x[2:])
    q_y = [rcopy(cot.at[0:XC, token_cols(k)], qf.at[SLOT[k]], q_s.at[k], q_r.at[k], y_dev[NY - k]) for k in (1, 3, 2)]
    start(q_y)
    gc.wait()
    for p in range(PIECES):
        for i in range(NZ - 1):
            lt[p * PR : (p + 1) * PR, i * 128 : (i + 1) * 128] = gl[p // NX, p % NX, i]
    wait(od)
    for p in range(PIECES):
        for i in range(NZ - 1):
            lt[XR + p * PO : XR + (p + 1) * PO, i * 128 : (i + 1) * 128] = ol[p // NX, p % NX, i, 0:PO, :]
    lefts = [lt[b * RANK : (b + 1) * RANK, :] for b in range(NB)]
    inverses = inverse_factors([nt(left, left, PRECISE) for left in lefts])
    for b in range(NB):
        bas[b * RANK : (b + 1) * RANK, :] = nn(inverses[b], lefts[b], PRECISE)

    grads_x(1)
    grads_x(3)
    qf[0] = cot[0:XC, token_cols(0)]
    for i in range(2):
        hi, mid, _ = split3(bas[i * RANK : (i + 2) * RANK, :])
        terms = jnp.concatenate([hi, hi, mid, mid], axis=0).astype(F32)
        bav[i] = terms.T.astype(BF16)
    out_ba = pltpu.make_async_copy(bav, BA, st.at[3])
    out_ba.start()

    rpart[...] = nt(bas[...], acc[...], PRECISE)
    bas2 = jnp.concatenate(split3(bas[...])[:2], axis=0)

    def last_rows(first, size):
        part = nt(bas2, xg[2, first : first + size, :])
        part = jnp.concatenate(split3(part[:NR] + part[NR:])[:2], axis=0)
        begin = ((y + NY - 2) % NY) * ROWS + first
        part = nt(part, cot[0:XC, pl.ds(pl.multiple_of(begin, 128), size)])
        rpart[:, 0:XC] += part[:NR] + part[NR:]

    wait(fwd_x[:2])
    last_rows(0, CHR)
    last_rows(3 * CHR, CHR)
    wait(fwd_x[2:])
    last_rows(CHR, 2 * CHR)
    right = jnp.where(in_block((NR, PACK)), rpart[...] * scale, 0.0)
    packed = right[:RANK] + right[RANK : 2 * RANK] + right[2 * RANK :]
    hr = RANK // NC
    for e in range(NC):
        for i in range(NX):
            q1[e, i] = packed[e * hr : (e + 1) * hr, i * 128 : (i + 1) * 128]
    r1 = [rcopy(q1.at[(c + e) % NC, (x + k) % NX], rxr.at[e, k], r_s.at[0, e, k], r_r.at[0, e, k], row_dev[e, k])
          for e, k in row]
    start(r1)
    grads_x(2)
    wait(r1)
    mine = q1[c, x]
    for e, k in row:
        mine = mine + rxr[e, k]
    q2[...] = mine
    r2 = [rcopy(q2, rzr.at[k], z_s.at[2, k], z_r.at[2, k], z_dev[k]) for k in (4, 3, 5, 2, 6, 1, 7)]
    start(r2)
    nev[...] = acc[...].T * scale - tn(bas[...], right, PRECISE)
    out_ne = pltpu.make_async_copy(nev, NE, st.at[2])
    out_ne.start()
    wait(r2)
    rzr[0] = q2[...]
    total = rzr[z % NZ]
    for i in range(1, NZ):
        total = total + rzr[(z + NZ - i) % NZ]
    gr[c, x] = total
    r3 = [rcopy(gr.at[c, x], GR.at[c, x], r_s.at[1, e, k], r_r.at[1, e, k], row_dev[e, k]) for e, k in row]
    start(r3)
    out_gr = pltpu.make_async_copy(gr.at[c, x], GR.at[c, x], st.at[4])
    out_gr.start()

    w_c.wait()
    wait(q_y[:2])
    near = NY - 1
    gacc[...] = tn(qf[0:near].reshape(near * XC, ROWS), wf[0:near].reshape(near * XC, WL)[:, :D])
    q_y[2].wait()
    giv[...] = (gacc[...] + tn(qf[near], wf[near, :, 0:D])).astype(BF16)
    out_gi = pltpu.make_async_copy(giv, GI, st.at[0])
    out_gi.start()
    wait(r3)
    wait((out_gc, out_ne, out_ba, out_gi, out_gr))


def finish(GI, GC, NE, BA, GR, gi_out, gc_out, ne_out, cg_out, gi, gc, ne, ba, gr, cg, sem):
    loads = [
        pltpu.make_async_copy(a, b, sem.at[i])
        for i, (a, b) in enumerate(((GR, gr), (BA, ba), (NE, ne), (GI, gi), (GC, gc)))
    ]
    for cp in loads:
        cp.start()
    loads[0].wait()
    hr = RANK // NC
    col = lax.broadcasted_iota(jnp.int32, (RANK, 256), 1)
    rhs = []
    for i, edge in ((0, QC), (1, XC - 256)):
        total = jnp.concatenate(
            [jnp.concatenate([gr[e, 2 * i], gr[e, 2 * i + 1]], axis=1) for e in range(NC)], axis=0
        )
        total = jnp.concatenate([jnp.where(col < edge, total, 0.0), jnp.where(col < edge, 0.0, total)], axis=0)
        hi, mid, _ = split3(total)
        rhs.append(jnp.concatenate([hi, mid, hi, mid], axis=0))
    loads[1].wait()
    stores = []

    def store(src, dst):
        cp = pltpu.make_async_copy(src, dst, sem.at[5 + len(stores)])
        cp.start()
        stores.append(cp)

    half = D // 2
    for r in range(2):
        rows = pl.ds(r * half, half)
        for i in range(2):
            cg[rows, i * 256 : (i + 1) * 256] = nn(ba[i, rows, :], rhs[i])
        store(cg.at[rows], cg_out.at[rows])
    for cp, src, dst in zip(loads[2:], (ne, gi, gc), (ne_out, gi_out, gc_out)):
        cp.wait()
        store(src, dst)
    for cp in stores:
        cp.wait()


def on_device(
    normed_input, grad_query, grad_key, grad_value, context, grad_output,
    w_query, w_key, w_value, w_output, error, factor_init,
):
    any_spec = pl.BlockSpec(memory_space=pl.ANY)
    V = pltpu.VMEM
    hr = RANK // NC
    scratch = [
        V((NY, ROWS, D), BF16), V((NY, ROWS, D), BF16), V((PACK, TOK), BF16),
        V((QC, D), BF16), V((D, PACK), F32), V((RANK, PACK), F32),
        V((NY, XC, WL), BF16), V((NY, XC, ROWS), BF16), V((PACK, D), F32),
        V((NY, XR, ROWS), F32), V((NY, XR, ROWS), F32),
        V((PIECES, NY * PR, D), F32), V((NX, NY * PR, D), F32), V((NX, NY * PR, D), F32),
        V((NX, NY * PR, D), F32), V((NZ, NY * PR, 128), F32), V((NZ, NY * PR, 128), F32),
        V((NY, PR, 128), F32), V((NY, PR, 128), F32), V((NC, NX, NZ, PR, 128), F32),
        V((NR, D), F32), V((NR, D), F32),
        V((NC, NX, 8, D), F32), V((NC, NX, 8, D), F32), V((NZ, 8, 128), F32), V((NZ, 8, 128), F32),
        V((NC, NX, NZ, 8, 128), F32),
        V((NR, PACK), F32), V((NC, NX, hr, 128), F32), V((NC, NX, hr, 128), F32),
        V((hr, 128), F32), V((NZ, hr, 128), F32), V((NC, NX, hr, 128), F32),
        V((ROWS, D), F32), V((ROWS, D), BF16), V((QC, TOK), BF16), V((D, PACK), F32), V((2, D, 256), BF16),
    ]
    S = pltpu.SemaphoreType.DMA
    sems = [
        S((12,)), S((5,)), S((2, 4, CH)), S((2, 4, CH)), S((2, CH)), S((2, CH)), S((NY,)), S((NY,)),
        S((5,)), S((5,)), S((4, NX)), S((4, NX)), S((5, NZ)), S((5, NZ)),
        S((NX,)), S((NX,)), S((2, NY)), S((2, NY)), S((NY,)), S((NY,)),
        S((4, NC, NX)), S((4, NC, NX)),
    ]
    outs = (
        jax.ShapeDtypeStruct((ROWS, D), BF16),
        jax.ShapeDtypeStruct((QC, TOK), BF16),
        jax.ShapeDtypeStruct((D, PACK), F32),
    )
    parts = pl.pallas_call(
        body,
        out_shape=outs[:3] + (
            jax.ShapeDtypeStruct((2, D, 256), BF16),
            jax.ShapeDtypeStruct((NC, NX, hr, 128), F32),
        ),
        in_specs=[any_spec] * 12,
        out_specs=(any_spec,) * 5,
        scratch_shapes=scratch + sems,
        compiler_params=pltpu.CompilerParams(
            collective_id=0, has_side_effects=True, vmem_limit_bytes=60 * 2**20
        ),
        name="backward",
    )(
        normed_input, grad_query.T, grad_key.T, grad_value.T, context.T, grad_output,
        w_query.T, w_key.T, w_value.T, w_output, error, factor_init.T,
    )
    grad_input, grad_context, new_error, compressed = pl.pallas_call(
        finish,
        out_shape=outs + (jax.ShapeDtypeStruct((D, PACK), F32),),
        in_specs=[any_spec] * 5,
        out_specs=(any_spec,) * 4,
        scratch_shapes=[
            V((ROWS, D), BF16), V((QC, TOK), BF16), V((D, PACK), F32),
            V((2, D, 256), BF16), V((NC, NX, hr, 128), F32), V((D, PACK), F32), S((10,)),
        ],
        compiler_params=pltpu.CompilerParams(vmem_limit_bytes=60 * 2**20),
        name="finish",
    )(*parts)
    return grad_input, grad_context.T, new_error, compressed


def solution(mesh):
    return jax.shard_map(
        on_device,
        mesh=mesh,
        in_specs=(
            P(("dp", "tensor"), None),
            P("dp", "tensor"),
            P("dp", "tensor"),
            P("dp", "tensor"),
            P("dp", "tensor"),
            P(("dp", "tensor"), None),
            P(None, "tensor"),
            P(None, "tensor"),
            P(None, "tensor"),
            P("tensor", None),
            P("dp", "tensor"),
            P("tensor", None),
        ),
        out_specs=(
            P(("dp", "tensor"), None),
            P("dp", "tensor"),
            P("dp", "tensor"),
            P(None, "tensor"),
        ),
        check_vma=False,
    )
```
